32 devices in a mesh: pb: 8 (over z, y), slab: 4 (over x, core).
Axes of the slice: x: 2, y: 2, z: 4, core: 2. Of those that a mesh axis runs over, the one named last changes fastest.
Arguments:
- query_feats: bfloat16 [8, 128, 9, 256], P('pb', 'slab'), may hold values from -1.5 to 1.5
- frame_store: bfloat16 [32, 128, 9, 256], P(None, 'pb'), may hold values from -1.5 to 1.5
- candidates: int32 [8, 4], replicated, may hold values from 0 to 31
- query_length: int32 [8], P('pb'), may hold values from 16 to 128, as said below
- clip_length: int32 [32], replicated, may hold values from 16 to 128, as said below
- kernel_one: float32 [3, 3, 1, 32], replicated, may hold values from -2 to 2
- bias_one: float32 [32], replicated, may hold values from -0.2 to 0.2
- kernel_two: float32 [3, 3, 32, 64], replicated, may hold values from -0.375 to 0.375
- bias_two: float32 [64], replicated, may hold values from -0.2 to 0.2
- kernel_three: float32 [3, 3, 64, 128], replicated, may hold values from -0.25 to 0.25
- bias_three: float32 [128], replicated, may hold values from -0.2 to 0.2
- kernel_four: float32 [1, 1, 128, 1], replicated, may hold values from -0.5 to 0.5
- bias_four: float32 [1], replicated, may hold values from -1.75 to 1.75
Outputs:
- scores: float32 [8, 4], P('pb')
The draws below stay inside these ranges and needn't reach their ends.
Inputs may be any that keep to these rules, and one draw needn't show every extreme that they name: `query_length`: some query has exactly 128 valid frames and some exactly 16. `clip_length`: some candidate clip has exactly 128 valid frames and some exactly 16.
All inputs are finite; a program needn't handle non-finite values.
Results may differ from the reference program's by a relative error of at most 0.0003.
Values may be sent and summed in bfloat16 or wider, within the bound.
No kernel may reach another device: no remote copies, remote signals or barrier semaphores. Data moves between devices by JAX's collectives and lax.ppermute only.
A program may use at most 128 MiB of HBM per device.

```python
import jax
import jax.numpy as jnp
from jax import lax

F = 128
R = 9
C = 256
K1 = 32
K2 = 64
K3 = 128
P_SIZE = 4
QUERIES = 8
CLIPS = 32


def draw_bounded(key, amount, lowest, highest):
    keys = jax.random.split(key, 3)
    values = jax.random.randint(keys[0], (amount,), lowest, highest + 1)
    place_high = jax.random.randint(keys[1], (), 0, amount)
    place_low = (place_high + jax.random.randint(keys[2], (), 1, amount)) % amount
    values = values.at[place_high].set(highest)
    values = values.at[place_low].set(lowest)
    return values.astype(jnp.int32)


def draw_query_length(key, part):
    return draw_bounded(jax.random.fold_in(key, 11), QUERIES, 16, F)


def draw_clip_length(key, part):
    return draw_bounded(jax.random.fold_in(key, 23), CLIPS, 16, F)


def place_ends(values, key, low, largest):
    longest = values.shape.index(max(values.shape))
    spots = []
    for shift in (0, 1):
        where = [jax.random.randint(jax.random.fold_in(key, axis), (), 0, length) for axis, length in enumerate(values.shape)]
        where[longest] = (where[longest] + shift) % values.shape[longest]
        spots.append(tuple(where))
    return values.at[spots[0]].set(low).at[spots[1]].set(largest)


def levels(stream_key, extent, cuts, least, largest):
    level = 1.0
    for position, parts in cuts:
        draws = jax.random.uniform(jax.random.fold_in(jax.random.fold_in(stream_key, 6), position), (parts,), jnp.float32, least / len(cuts), largest / len(cuts))
        level = level * jnp.repeat(jnp.exp(draws), extent[position] // parts).reshape((-1,) + (1,) * (len(extent) - 1 - position))
    return level


def noise(rng, shape, deviation, reach, cuts=(), held_as=jnp.bfloat16):
    entries = deviation * jax.random.normal(rng, shape, jnp.float32)
    if cuts:
        entries = entries * levels(rng, shape, cuts, -0.22, 0.18)
    return jnp.clip(entries, -reach, reach).astype(held_as)


def setup_inputs(seed: int = 0) -> dict:
    key_of = jax.random.split(jax.random.key(seed), 14)
    query_feats = noise(key_of[0], (QUERIES, F, R, C), (C ** 0.5) ** -0.5, 1.5, ((0, 8), (1, 4)))
    frame_store = noise(key_of[1], (CLIPS, F, R, C), (C ** 0.5) ** -0.5, 1.5, ((1, 8),))
    candidates = place_ends(jax.random.randint(key_of[2], (QUERIES, P_SIZE), 0, CLIPS), jax.random.fold_in(key_of[2], 1), 0, CLIPS - 1).astype(jnp.int32)
    query_length = draw_query_length(jax.random.fold_in(key_of[13], 71), 0)
    clip_length = draw_clip_length(jax.random.fold_in(key_of[13], 71), 0)
    kernel_one = noise(key_of[5], (3, 3, 1, K1), 9 ** -0.5, 2.0, (), jnp.float32)
    bias_one = jnp.clip(jax.random.uniform(key_of[6], (K1,), jnp.float32, -0.2, 0.2), -0.2, 0.2)
    kernel_two = noise(key_of[7], (3, 3, K1, K2), (9 * K1) ** -0.5, 0.375, (), jnp.float32)
    bias_two = jnp.clip(jax.random.uniform(key_of[8], (K2,), jnp.float32, -0.2, 0.2), -0.2, 0.2)
    kernel_three = noise(key_of[9], (3, 3, K2, K3), (9 * K2) ** -0.5, 0.25, (), jnp.float32)
    bias_three = jnp.clip(jax.random.uniform(key_of[10], (K3,), jnp.float32, -0.2, 0.2), -0.2, 0.2)
    kernel_four = noise(key_of[11], (1, 1, K3, 1), K3 ** -0.5, 0.5, (), jnp.float32)
    bias_four = noise(key_of[12], (1,), 0.3, 1.75, (), jnp.float32)
    return {"query_feats": query_feats, "frame_store": frame_store, "candidates": candidates, "query_length": query_length, "clip_length": clip_length, "kernel_one": kernel_one, "bias_one": bias_one, "kernel_two": kernel_two, "bias_two": bias_two, "kernel_three": kernel_three, "bias_three": bias_three, "kernel_four": kernel_four, "bias_four": bias_four}


def region_map(features, clip):
    feature_width = features.shape[-1]
    gram = lax.dot_general(features.reshape(-1, feature_width), clip.reshape(-1, feature_width), (((1,), (1,)), ((), ())), preferred_element_type=jnp.float32)
    gram = gram.reshape(features.shape[0], features.shape[1], clip.shape[0], clip.shape[1])
    return jnp.mean(jnp.max(gram, axis=3), axis=1)


def conv_same(field, kernel, bias):
    result = lax.conv_general_dilated(field, kernel, (1, 1), ((1, 1), (1, 1)), dimension_numbers=("NHWC", "HWIO", "NHWC"), precision=lax.Precision.HIGHEST)
    return result + bias


def point_conv(field, kernel, bias):
    result = jnp.einsum("nhwk,ko->nhwo", field, kernel[0, 0], precision=lax.Precision.HIGHEST)
    return result + bias


def pool_pairs(field):
    shape_now = field.shape
    blocks = field.reshape(shape_now[0], shape_now[1] // 2, 2, shape_now[2] // 2, 2, shape_now[3])
    return jnp.max(blocks, axis=(2, 4))


def reference(query_feats, frame_store, candidates, query_length, clip_length, kernel_one, bias_one, kernel_two, bias_two, kernel_three, bias_three, kernel_four, bias_four):
    positions = jnp.arange(F, dtype=jnp.int32)
    pooled = jnp.arange(F // 4, dtype=jnp.int32)

    def per_query(packed):
        features, length_now, clip_ids = packed
        clips = frame_store[clip_ids]

        def single_clip(clip):
            return region_map(features, clip)

        maps = lax.map(single_clip, clips)
        pair_length = clip_length[clip_ids]
        row_valid = positions < length_now
        col_valid = positions[None, :] < pair_length[:, None]
        masked = jnp.where(row_valid[None, :, None] & col_valid[:, None, :], maps, 0.0)
        layer_one = pool_pairs(jax.nn.relu(conv_same(masked[..., None], kernel_one, bias_one)))
        layer_two = pool_pairs(jax.nn.relu(conv_same(layer_one, kernel_two, bias_two)))
        layer_three = jax.nn.relu(conv_same(layer_two, kernel_three, bias_three))
        final_maps = jnp.clip(point_conv(layer_three, kernel_four, bias_four)[..., 0], -1.0, 1.0)
        col_keep = 4 * pooled[None, :] < pair_length[:, None]
        row_keep = 4 * pooled < length_now
        row_best = jnp.max(jnp.where(col_keep[:, None, :], final_maps, -2.0), axis=2)
        row_total = jnp.sum(jnp.where(row_keep[None, :], row_best, 0.0), axis=1)
        row_number = ((length_now + 3) // 4).astype(jnp.float32)
        return row_total / row_number

    return lax.map(per_query, (query_feats, query_length, candidates))
```

```python
import functools

import jax
import jax.numpy as jnp
from jax import lax
from jax.experimental import pallas as pl
from jax.experimental.pallas import tpu as pltpu
from jax.sharding import PartitionSpec as P

F32 = jnp.float32
BF16 = jnp.bfloat16
LANES = 128


def exchange_rounds(count, core):
    half = count // 2
    far = list(range(count - 1, half - 1, -1))
    near = list(range(half - 1, 0, -1))
    return far + near if core == 0 else near + far


def split(x):
    high = x.astype(BF16)
    return high, (x - high.astype(F32)).astype(BF16)


def pick_kernel(rounds, cand_ref, store_ref, *rest):
    outs, sem = rest[:-1], rest[-1]
    query = lax.axis_index("pb")
    pair = lax.axis_index("slab")
    odd = lax.rem(pair, 2)
    copies = []
    for at, out in enumerate(outs):
        if at < len(rounds[0]):
            target = query ^ jnp.where(odd == 0, rounds[0][at], rounds[1][at])
        else:
            target = query
        copy = pltpu.make_async_copy(store_ref.at[cand_ref[target, pair]], out, sem.at[at])
        copy.start()
        copies.append(copy)
    for copy in copies:
        copy.wait()


def weight_kernel(one_ref, two_ref, three_ref, w1_ref, w2a_ref, w2b_ref, w3a_ref, w3b_ref):
    def place(ref, base, value):
        rows = value.shape[0]
        span = ref.shape[0] // 3
        high, low = split(value)
        ref[pl.ds(base, rows), :] = high
        ref[pl.ds(span + base, rows), :] = high
        ref[pl.ds(2 * span + base, rows), :] = low

    def iotas(rows):
        return (
            lax.broadcasted_iota(jnp.int32, (rows, 256), 0),
            lax.broadcasted_iota(jnp.int32, (rows, 256), 1),
        )

    row, lane = iotas(LANES)
    group = lane // 32
    column = 2 * (group % 4) + group // 4
    total = jnp.zeros((LANES, 256), F32)
    for d in range(3):
        for t in range(3):
            mask = (row // 16 == d) & (row % 16 - column == t)
            total = jnp.where(mask, one_ref[3 * d + t : 3 * d + t + 1, :], total)
    place(w1_ref, 0, total)

    group = lane // 64
    column = 2 * (group % 2) + group // 2
    for ref, first in ((w2a_ref, 0), (w2b_ref, 4)):
        for d in range(3):
            total = jnp.zeros((LANES, 256), F32)
            for t in range(3):
                tile = two_ref[3 * d + t]
                total = jnp.where(row // 32 + first - column == t, jnp.concatenate([tile] * 4, axis=0), total)
            place(ref, LANES * d, total)

    column = lane // 128
    for ref, first in ((w3a_ref, 0), (w3b_ref, 2)):
        for d in range(3):
            total = jnp.zeros((LANES, 256), F32)
            for t in range(3):
                tile = three_ref[3 * d + t]
                total = jnp.where(row // 64 + first - column == t, jnp.concatenate([tile] * 2, axis=0), total)
            place(ref, LANES * d, total)


def moved_rows(x, step):
    rows = x.shape[0]
    row = lax.broadcasted_iota(jnp.int32, x.shape, 0)
    if step == 1:
        return jnp.where(row == 0, 0.0, pltpu.roll(x, 1, 0))
    return jnp.where(row == rows - 1, 0.0, pltpu.roll(x, rows - 1, 0))


def dot(a, b):
    return jnp.dot(a, b, preferred_element_type=F32)


def score_kernel(
    rounds,
    n_blocks,
    n_slabs,
    regions,
    frames,
    cand_ref,
    qlen_ref,
    clen_ref,
    *rest,
):
    blocks = rest[:n_blocks]
    slabs = rest[n_blocks : n_blocks + n_slabs]
    (
        w1_ref,
        w2a_ref,
        w2b_ref,
        w3a_ref,
        w3b_ref,
        b1_ref,
        b2_ref,
        b3_ref,
        k4_ref,
        b4_ref,
        out_ref,
        clip,
        feats,
        best,
        sim,
        x1,
        x2,
        x3,
    ) = rest[n_blocks + n_slabs :]
    query = lax.axis_index("pb")
    pair = lax.axis_index("slab")
    odd = lax.rem(pair, 2)
    feature_width = feats.shape[-1]
    query_len = qlen_ref[0]
    clip_len = clen_ref[cand_ref[query, pair]]

    if n_blocks == 1:
        clip[...] = blocks[0][...]
    else:
        for at, block in enumerate(blocks):
            band = block.shape[1]
            source = query
            if at < n_blocks - 1:
                source = query ^ jnp.where(odd == 0, rounds[0][at], rounds[1][at])
            clip[:, pl.ds(pl.multiple_of(source * band, band), band), :] = block[...]
    for k, slab in enumerate(slabs):
        rows = slab.shape[1]
        feats[:, pl.ds(pl.multiple_of((pair ^ k) * rows, rows), rows), :] = slab[...]

    flat = feats[...].reshape(regions * frames, feature_width)
    for s in range(0, regions, 2):
        width = min(2, regions - s)
        part = clip[s : s + width].reshape(width * frames, feature_width)
        gram = lax.dot_general(flat, part, (((1,), (1,)), ((), ())), preferred_element_type=F32)
        if width == 2:
            gram = jnp.maximum(gram[:, :frames], gram[:, frames:])
        best[...] = gram if s == 0 else jnp.maximum(best[...], gram)
    total = best[0:frames, :]
    for r in range(1, regions):
        total = total + best[r * frames : (r + 1) * frames, :]
    row = lax.broadcasted_iota(jnp.int32, (frames, frames), 0)
    col = lax.broadcasted_iota(jnp.int32, (frames, frames), 1)
    sim[...] = jnp.where((row < query_len) & (col < clip_len), total * (1.0 / regions), 0.0)

    quarter = frames // 4
    phases = [sim[pl.ds(p, quarter, stride=4), :] for p in range(4)]
    ordered = jnp.concatenate([moved_rows(phases[3], 1), *phases, moved_rows(phases[0], -1)], axis=0)
    windows = frames // 8
    rolled = [pltpu.roll(ordered, 8 * m + 1, 1) for m in range(16)]
    lane = lax.broadcasted_iota(jnp.int32, (frames, LANES), 1)
    for n in range(windows):
        taps = [rolled[(2 * d - n) % 16][d * quarter : d * quarter + frames] for d in range(3)]
        field = jnp.where(lane < 16, taps[0], jnp.where(lane < 32, taps[1], taps[2]))
        if n == 0:
            field = jnp.where(lane % 16 == 0, 0.0, field)
        if n == windows - 1:
            field = jnp.where(lane % 16 == 9, 0.0, field)
        high, low = split(field)
        x1[n * frames : (n + 1) * frames, 0:LANES] = high
        x1[n * frames : (n + 1) * frames, LANES : 2 * LANES] = low
    made = dot(x1[...], w1_ref[0:256, :]) + dot(x1[:, 0:LANES], w1_ref[256:384, :])
    made = jnp.maximum(made[:, :LANES], made[:, LANES:])
    first = []
    for n in range(windows):
        here = made[n * frames : (n + 1) * frames]
        halves = []
        for e in range(2):
            pooled = jnp.maximum(
                here[2 * e * quarter : (2 * e + 1) * quarter], here[(2 * e + 1) * quarter : (2 * e + 2) * quarter]
            )
            halves.append(jnp.maximum(pooled + b1_ref[...], 0.0))
        first.append(halves)

    lane = lax.broadcasted_iota(jnp.int32, (quarter, LANES), 1)

    def shifted(parts, width):
        turned = [pltpu.roll(x, width, 1) for x in parts]
        result = []
        for n in range(len(parts) + 1):
            before = turned[n - 1] if n > 0 else jnp.zeros_like(turned[0])
            after = turned[n] if n < len(parts) else jnp.zeros_like(turned[0])
            result.append(jnp.where(lane < width, before, after))
        return result

    even = shifted([x[0] for x in first], 32)
    odds = shifted([x[1] for x in first], 32)
    half = 2 * quarter
    for n in range(windows + 1):
        base = n * half
        e = split(even[n])
        o = split(odds[n])
        down = split(moved_rows(odds[n], 1))
        up = split(moved_rows(even[n], -1))
        for d, (top, bottom) in enumerate(((down, e), (e, o), (o, up))):
            for part in range(2):
                at = part * 3 * LANES + d * LANES
                x2[base : base + quarter, at : at + LANES] = top[part]
                x2[base + quarter : base + half, at : at + LANES] = bottom[part]
    rows = windows * half
    made = (
        dot(x2[0:rows, :], w2a_ref[0:768, :])
        + dot(x2[0:rows, 0:384], w2a_ref[768:1152, :])
        + dot(x2[half : half + rows, :], w2b_ref[0:768, :])
        + dot(x2[half : half + rows, 0:384], w2b_ref[768:1152, :])
    )
    made = jnp.maximum(made[:, :LANES], made[:, LANES:])
    second = []
    for n in range(windows):
        here = jnp.maximum(made[n * half : n * half + quarter], made[n * half + quarter : (n + 1) * half])
        second.append(jnp.maximum(here + b2_ref[...], 0.0))

    moved = shifted(second, 64)
    for n in range(windows + 1):
        base = n * quarter
        for d, value in enumerate((moved_rows(moved[n], 1), moved[n], moved_rows(moved[n], -1))):
            high, low = split(value)
            x3[base : base + quarter, d * LANES : (d + 1) * LANES] = high
            x3[base : base + quarter, (3 + d) * LANES : (4 + d) * LANES] = low
    rows = windows * quarter
    made = (
        dot(x3[0:rows, :], w3a_ref[0:768, :])
        + dot(x3[0:rows, 0:384], w3a_ref[768:1152, :])
        + dot(x3[quarter : quarter + rows, :], w3b_ref[0:768, :])
        + dot(x3[quarter : quarter + rows, 0:384], w3b_ref[768:1152, :])
    )
    made = jnp.maximum(made + b3_ref[...], 0.0) * k4_ref[...]
    bias_four = b4_ref[0]
    row_best = jnp.full((quarter, 1), -2.0, F32)
    for c in range(2):
        summed = jnp.sum(made[:, c * LANES : (c + 1) * LANES], axis=1, keepdims=True)
        final = jnp.clip(summed + bias_four, -1.0, 1.0)
        for n in range(windows):
            here = final[n * quarter : (n + 1) * quarter]
            keep = 4 * (2 * n + c) < clip_len
            row_best = jnp.maximum(row_best, jnp.where(keep, here, -2.0))
    row = lax.broadcasted_iota(jnp.int32, (quarter, 1), 0)
    kept = jnp.where(4 * row < query_len, row_best, 0.0)
    number = jnp.broadcast_to(((query_len + 3) // 4).astype(F32), (1, 1))
    score = jnp.sum(kept, axis=0, keepdims=True) / number
    lane = lax.broadcasted_iota(jnp.int32, out_ref.shape, 1)
    out_ref[...] = jnp.where(lane == pair, score, 0.0)


def per_device(
    query_feats,
    frame_store,
    candidates,
    query_length,
    clip_length,
    kernel_one,
    bias_one,
    kernel_two,
    bias_two,
    kernel_three,
    bias_three,
    kernel_four,
    bias_four,
):
    slab_rows, regions, feature_width = query_feats.shape[1:]
    band = frame_store.shape[1]
    n_query = lax.axis_size("pb")
    n_slab = lax.axis_size("slab")
    frames = band * n_query
    pair_count = candidates.shape[1]
    assert pair_count == n_slab and slab_rows * n_slab == frames == LANES
    vmem = pl.BlockSpec(memory_space=pltpu.VMEM)
    smem = pl.BlockSpec(memory_space=pltpu.SMEM)
    anywhere = pl.BlockSpec(memory_space=pl.ANY)
    store = jnp.transpose(frame_store, (0, 2, 1, 3))
    own = jnp.transpose(query_feats[0], (1, 0, 2))

    rounds = None
    if n_query <= 8:
        rounds = [exchange_rounds(n_query, core) for core in range(2)]
        sent = pl.pallas_call(
            functools.partial(pick_kernel, rounds),
            out_shape=[jax.ShapeDtypeStruct(store.shape[1:], BF16)] * n_query,
            in_specs=[smem, anywhere],
            out_specs=[anywhere] * n_query,
            scratch_shapes=[pltpu.SemaphoreType.DMA((n_query,))],
            name="pick_bands",
        )(candidates, store)
        blocks = []
        for at in range(n_query - 1):
            moves = [
                (q * n_slab + s, (q ^ rounds[s % 2][at]) * n_slab + s) for q in range(n_query) for s in range(n_slab)
            ]
            blocks.append(lax.ppermute(sent[at], ("pb", "slab"), moves))
        blocks.append(sent[n_query - 1])
    else:
        ids = lax.dynamic_index_in_dim(candidates, lax.axis_index("slab"), 1, keepdims=False)
        got = lax.all_to_all(store[ids], "pb", 0, 0, tiled=True)
        blocks = [jnp.transpose(got, (1, 0, 2, 3)).reshape(regions, frames, feature_width)]
    slabs = [own]
    for k in range(1, n_slab):
        slabs.append(lax.ppermute(own, "slab", [(s, s ^ k) for s in range(n_slab)]))

    one = jnp.tile(kernel_one.reshape(9, -1), (1, 8))
    two = jnp.tile(kernel_two.reshape(9, 32, 64), (1, 1, 4))
    three = jnp.tile(kernel_three.reshape(9, 64, 128), (1, 1, 2))
    weights = pl.pallas_call(
        weight_kernel,
        out_shape=[jax.ShapeDtypeStruct((384, 256), BF16)] + [jax.ShapeDtypeStruct((1152, 256), BF16)] * 4,
        in_specs=[vmem] * 3,
        out_specs=[vmem] * 5,
        cost_estimate=pl.CostEstimate(flops=2_000_000, bytes_accessed=6_000_000, transcendentals=0),
        name="lay_out_kernels",
    )(one, two, three)

    vector = pl.pallas_call(
        functools.partial(score_kernel, rounds, len(blocks), n_slab, regions, frames),
        out_shape=jax.ShapeDtypeStruct((1, LANES), F32),
        in_specs=[smem] * 3 + [vmem] * (len(blocks) + n_slab + 9) + [smem],
        out_specs=vmem,
        scratch_shapes=[
            pltpu.VMEM((regions, frames, feature_width), BF16),
            pltpu.VMEM((regions, frames, feature_width), BF16),
            pltpu.VMEM((regions * frames, frames), F32),
            pltpu.VMEM((frames, frames), F32),
            pltpu.VMEM((16 * frames, 256), BF16),
            pltpu.VMEM((17 * 64, 768), BF16),
            pltpu.VMEM((17 * 32, 768), BF16),
        ],
        compiler_params=pltpu.CompilerParams(vmem_limit_bytes=40 * 1024 * 1024),
        cost_estimate=pl.CostEstimate(flops=2_000_000_000, bytes_accessed=8_000_000, transcendentals=0),
        name="score_pair",
    )(
        candidates,
        query_length,
        clip_length,
        *blocks,
        *slabs,
        *weights,
        jnp.tile(bias_one, 4)[None],
        jnp.tile(bias_two, 2)[None],
        jnp.tile(bias_three, 2)[None],
        jnp.tile(kernel_four.reshape(-1), 2)[None],
        bias_four,
    )
    for k in (1, 2):
        vector = vector + lax.ppermute(vector, "slab", [(s, s ^ k) for s in range(n_slab)])
    return vector[:, :pair_count]


def solution(mesh):
    placed = (
        P("pb", "slab", None, None),
        P(None, "pb", None, None),
        P(),
        P("pb"),
        P(),
        P(),
        P(),
        P(),
        P(),
        P(),
        P(),
        P(),
        P(),
    )
    return jax.shard_map(
        per_device, mesh=mesh, in_specs=placed, out_specs=P("pb", None), check_vma=False
    )
```

```python
import functools

import jax
import jax.numpy as jnp
from jax import lax
from jax.experimental import pallas as pl
from jax.experimental.pallas import tpu as pltpu
from jax.sharding import PartitionSpec as P

F32 = jnp.float32
BF16 = jnp.bfloat16
LANES = 128


def exchange_rounds(count):
    odd, even = list(range(count - 1, 1, -2)), list(range(count - 2, 1, -2))
    return odd, even[-1:] + even[:-1]


def split(x):
    high = x.astype(BF16)
    return high, (x - high.astype(F32)).astype(BF16)


def pick_kernel(rounds, cand_ref, store_ref, *rest):
    outs, sem = rest[:-1], rest[-1]
    query = lax.axis_index("pb")
    pair = lax.axis_index("slab")
    odd = lax.rem(pair, 2)
    steps = len(rounds[0])
    copies = []
    for at, out in enumerate(outs):
        if at < steps:
            target = query ^ jnp.where(odd == 0, rounds[0][at], rounds[1][at])
            for part in range(2):
                clip = cand_ref[pair ^ part, target]
                copies.append(pltpu.make_async_copy(store_ref.at[clip], out.at[part], sem.at[2 * at + part]))
        else:
            clip = cand_ref[pair, query ^ (steps + 1 - at)]
            copies.append(pltpu.make_async_copy(store_ref.at[clip], out, sem.at[steps + at]))
    for copy in copies:
        copy.start()
    for copy in copies:
        copy.wait()


def weight_kernel(one_ref, two_ref, three_ref, w1_ref, w2a_ref, w2b_ref, w3a_ref, w3b_ref):
    def place(ref, base, value):
        rows = value.shape[0]
        span = ref.shape[0] // 3
        high, low = split(value)
        ref[pl.ds(base, rows), :] = high
        ref[pl.ds(span + base, rows), :] = high
        ref[pl.ds(2 * span + base, rows), :] = low

    def iotas(rows):
        return (
            lax.broadcasted_iota(jnp.int32, (rows, 256), 0),
            lax.broadcasted_iota(jnp.int32, (rows, 256), 1),
        )

    def wide(x, times):
        while times > 1:
            x = jnp.concatenate([x, x], axis=1)
            times //= 2
        return x

    row, lane = iotas(LANES)
    group = lane // 32
    column = 2 * (group % 4) + group // 4
    total = jnp.zeros((LANES, 256), F32)
    for d in range(3):
        for t in range(3):
            mask = (row // 16 == d) & (row % 16 - column == t)
            total = jnp.where(mask, wide(one_ref[3 * d + t], 8), total)
    place(w1_ref, 0, total)

    group = lane // 64
    column = 2 * (group % 2) + group // 2
    for ref, first in ((w2a_ref, 0), (w2b_ref, 4)):
        for d in range(3):
            total = jnp.zeros((LANES, 256), F32)
            for t in range(3):
                tile = jnp.concatenate([wide(two_ref[3 * d + t], 4)] * 4, axis=0)
                total = jnp.where(row // 32 + first - column == t, tile, total)
            place(ref, LANES * d, total)

    column = lane // 128
    for ref, first in ((w3a_ref, 0), (w3b_ref, 2)):
        for d in range(3):
            total = jnp.zeros((LANES, 256), F32)
            for t in range(3):
                tile = jnp.concatenate([wide(three_ref[3 * d + t], 2)] * 2, axis=0)
                total = jnp.where(row // 64 + first - column == t, tile, total)
            place(ref, LANES * d, total)


def moved_rows(x, step):
    rows = x.shape[0]
    row = lax.broadcasted_iota(jnp.int32, x.shape, 0)
    if step == 1:
        return jnp.where(row == 0, 0.0, pltpu.roll(x, 1, 0))
    return jnp.where(row == rows - 1, 0.0, pltpu.roll(x, rows - 1, 0))


def dot(a, b):
    return jnp.dot(a, b, preferred_element_type=F32)


def score_kernel(
    rounds,
    n_blocks,
    order,
    regions,
    frames,
    cand_ref,
    qlen_ref,
    clen_ref,
    *rest,
):
    blocks = rest[:n_blocks]
    n_slabs = len(order)
    slabs = rest[n_blocks : n_blocks + n_slabs]
    (
        w1_ref,
        w2a_ref,
        w2b_ref,
        w3a_ref,
        w3b_ref,
        b1_ref,
        b2_ref,
        b3_ref,
        k4_ref,
        b4_ref,
        out_ref,
        clip,
        feats,
        best,
        sim,
        x1,
        x2,
        x3,
    ) = rest[n_blocks + n_slabs :]
    query = lax.axis_index("pb")
    pair = lax.axis_index("slab")
    odd = lax.rem(pair, 2)
    feature_width = feats.shape[-1]
    query_len = qlen_ref[0]
    clip_len = clen_ref[cand_ref[pair, query]]

    if n_blocks == 1:
        clip[...] = blocks[0][...]
    else:
        steps = len(rounds[0])
        band = blocks[-1].shape[1]
        pieces = [(0, blocks[-1][...]), (1, blocks[-2][...])]
        for at in range(steps):
            first, second = rounds[0][at], rounds[1][at]
            pieces.append((jnp.where(odd == 0, first, second), blocks[at][0]))
            pieces.append((jnp.where(odd == 0, second, first), blocks[steps + at][1]))
        for k, value in pieces:
            clip[:, pl.ds(pl.multiple_of((query ^ k) * band, band), band), :] = value
    for k, slab in zip(order, slabs):
        rows = slab.shape[1]
        feats[:, pl.ds(pl.multiple_of((pair ^ k) * rows, rows), rows), :] = slab[...]

    flat = feats[...].reshape(regions * frames, feature_width)
    for s in range(0, regions, 2):
        width = min(2, regions - s)
        part = clip[s : s + width].reshape(width * frames, feature_width)
        gram = lax.dot_general(flat, part, (((1,), (1,)), ((), ())), preferred_element_type=F32)
        if width == 2:
            gram = jnp.maximum(gram[:, :frames], gram[:, frames:])
        best[...] = gram if s == 0 else jnp.maximum(best[...], gram)
    total = best[0:frames, :]
    for r in range(1, regions):
        total = total + best[r * frames : (r + 1) * frames, :]
    row = lax.broadcasted_iota(jnp.int32, (frames, frames), 0)
    col = lax.broadcasted_iota(jnp.int32, (frames, frames), 1)
    sim[...] = jnp.where((row < query_len) & (col < clip_len), total * (1.0 / regions), 0.0)

    quarter = frames // 4
    phases = [sim[pl.ds(p, quarter, stride=4), :] for p in range(4)]
    ordered = jnp.concatenate([moved_rows(phases[3], 1), *phases, moved_rows(phases[0], -1)], axis=0)
    windows = frames // 8
    rolled = [pltpu.roll(ordered, 8 * m + 1, 1) for m in range(16)]
    lane = lax.broadcasted_iota(jnp.int32, (frames, LANES), 1)
    for n in range(windows):
        taps = [rolled[(2 * d - n) % 16][d * quarter : d * quarter + frames] for d in range(3)]
        field = jnp.where(lane < 16, taps[0], jnp.where(lane < 32, taps[1], taps[2]))
        if n == 0:
            field = jnp.where(lane % 16 == 0, 0.0, field)
        if n == windows - 1:
            field = jnp.where(lane % 16 == 9, 0.0, field)
        high, low = split(field)
        x1[n * frames : (n + 1) * frames, 0:LANES] = high
        x1[n * frames : (n + 1) * frames, LANES : 2 * LANES] = low
    made = dot(x1[...], w1_ref[0:256, :]) + dot(x1[:, 0:LANES], w1_ref[256:384, :])
    made = jnp.maximum(made[:, :LANES], made[:, LANES:])
    bias_one = jnp.concatenate([b1_ref[...]] * 4, axis=1)
    bias_two = jnp.concatenate([b2_ref[...]] * 2, axis=1)
    first = []
    for n in range(windows):
        here = made[n * frames : (n + 1) * frames]
        halves = []
        for e in range(2):
            pooled = jnp.maximum(
                here[2 * e * quarter : (2 * e + 1) * quarter], here[(2 * e + 1) * quarter : (2 * e + 2) * quarter]
            )
            halves.append(jnp.maximum(pooled + bias_one, 0.0))
        first.append(halves)

    lane = lax.broadcasted_iota(jnp.int32, (quarter, LANES), 1)

    def shifted(parts, width):
        turned = [pltpu.roll(x, width, 1) for x in parts]
        result = []
        for n in range(len(parts) + 1):
            before = turned[n - 1] if n > 0 else jnp.zeros_like(turned[0])
            after = turned[n] if n < len(parts) else jnp.zeros_like(turned[0])
            result.append(jnp.where(lane < width, before, after))
        return result

    even = shifted([x[0] for x in first], 32)
    odds = shifted([x[1] for x in first], 32)
    half = 2 * quarter
    for n in range(windows + 1):
        base = n * half
        e = split(even[n])
        o = split(odds[n])
        down = split(moved_rows(odds[n], 1))
        up = split(moved_rows(even[n], -1))
        for d, (top, bottom) in enumerate(((down, e), (e, o), (o, up))):
            for part in range(2):
                at = part * 3 * LANES + d * LANES
                x2[base : base + quarter, at : at + LANES] = top[part]
                x2[base + quarter : base + half, at : at + LANES] = bottom[part]
    rows = windows * half
    made = (
        dot(x2[0:rows, :], w2a_ref[0:768, :])
        + dot(x2[0:rows, 0:384], w2a_ref[768:1152, :])
        + dot(x2[half : half + rows, :], w2b_ref[0:768, :])
        + dot(x2[half : half + rows, 0:384], w2b_ref[768:1152, :])
    )
    made = jnp.maximum(made[:, :LANES], made[:, LANES:])
    second = []
    for n in range(windows):
        here = jnp.maximum(made[n * half : n * half + quarter], made[n * half + quarter : (n + 1) * half])
        second.append(jnp.maximum(here + bias_two, 0.0))

    moved = shifted(second, 64)
    for n in range(windows + 1):
        base = n * quarter
        for d, value in enumerate((moved_rows(moved[n], 1), moved[n], moved_rows(moved[n], -1))):
            high, low = split(value)
            x3[base : base + quarter, d * LANES : (d + 1) * LANES] = high
            x3[base : base + quarter, (3 + d) * LANES : (4 + d) * LANES] = low
    rows = windows * quarter
    made = (
        dot(x3[0:rows, :], w3a_ref[0:768, :])
        + dot(x3[0:rows, 0:384], w3a_ref[768:1152, :])
        + dot(x3[quarter : quarter + rows, :], w3b_ref[0:768, :])
        + dot(x3[quarter : quarter + rows, 0:384], w3b_ref[768:1152, :])
    )
    bias_four = b4_ref[0]
    row_best = jnp.full((quarter, 1), -2.0, F32)
    for c in range(2):
        third = jnp.maximum(made[:, c * LANES : (c + 1) * LANES] + b3_ref[...], 0.0)
        summed = jnp.sum(third * k4_ref[...], axis=1, keepdims=True)
        final = jnp.clip(summed + bias_four, -1.0, 1.0)
        for n in range(windows):
            here = final[n * quarter : (n + 1) * quarter]
            keep = 4 * (2 * n + c) < clip_len
            row_best = jnp.maximum(row_best, jnp.where(keep, here, -2.0))
    row = lax.broadcasted_iota(jnp.int32, (quarter, 1), 0)
    kept = jnp.where(4 * row < query_len, row_best, 0.0)
    number = jnp.broadcast_to(((query_len + 3) // 4).astype(F32), (1, 1))
    score = jnp.sum(kept, axis=0, keepdims=True) / number
    lane = lax.broadcasted_iota(jnp.int32, out_ref.shape, 1)
    out_ref[...] = jnp.where(lane == pair, score, 0.0)


def per_device(
    query_feats,
    frame_store,
    candidates,
    query_length,
    clip_length,
    kernel_one,
    bias_one,
    kernel_two,
    bias_two,
    kernel_three,
    bias_three,
    kernel_four,
    bias_four,
):
    slab_rows, regions, feature_width = query_feats.shape[1:]
    band = frame_store.shape[1]
    n_query = lax.axis_size("pb")
    n_slab = lax.axis_size("slab")
    frames = band * n_query
    pair_count = candidates.shape[1]
    assert pair_count == n_slab and slab_rows * n_slab == frames == LANES
    vmem = pl.BlockSpec(memory_space=pltpu.VMEM)
    smem = pl.BlockSpec(memory_space=pltpu.SMEM)
    anywhere = pl.BlockSpec(memory_space=pl.ANY)
    store = jnp.transpose(frame_store, (0, 2, 1, 3))
    own = jnp.transpose(query_feats[0], (1, 0, 2))

    def swap(x, k):
        return lax.ppermute(x, "slab", [(s, s ^ k) for s in range(n_slab)])

    rounds = None
    if n_query == 8 and n_slab % 2 == 0:
        rounds = exchange_rounds(n_query)
        steps = len(rounds[0])
        sent = pl.pallas_call(
            functools.partial(pick_kernel, rounds),
            out_shape=[jax.ShapeDtypeStruct((2, *store.shape[1:]), BF16)] * steps
            + [jax.ShapeDtypeStruct(store.shape[1:], BF16)] * 2,
            in_specs=[smem, anywhere],
            out_specs=[vmem] * (steps + 2),
            scratch_shapes=[pltpu.SemaphoreType.DMA((2 * steps + 2,))],
            compiler_params=pltpu.CompilerParams(vmem_limit_bytes=2 * 1024 * 1024),
            name="pick_bands",
        )(candidates.T, store)
        near = []
        for at in range(steps):
            moves = [(q * n_slab + s, (q ^ rounds[s % 2][at]) * n_slab + s) for q in range(n_query) for s in range(n_slab)]
            near.append(lax.ppermute(sent[at], ("pb", "slab"), moves))
        one_away = lax.ppermute(sent[steps], "pb", [(q, q ^ 1) for q in range(n_query)])
        blocks = [*near, *[swap(x, 1) for x in near], one_away, sent[steps + 1]]
    else:
        ids = lax.dynamic_index_in_dim(candidates, lax.axis_index("slab"), 1, keepdims=False)
        got = lax.all_to_all(store[ids], "pb", 0, 0, tiled=True)
        blocks = [jnp.transpose(got, (1, 0, 2, 3)).reshape(regions, frames, feature_width)]
    slabs = [own]
    steps = [1 << i for i in range(n_slab.bit_length() - 1)]
    for k in reversed(steps):
        slabs = slabs + [swap(x, k) for x in slabs]
    order = [0]
    for k in reversed(steps):
        order = order + [o ^ k for o in order]

    weights = pl.pallas_call(
        weight_kernel,
        out_shape=[jax.ShapeDtypeStruct((384, 256), BF16)] + [jax.ShapeDtypeStruct((1152, 256), BF16)] * 4,
        in_specs=[vmem] * 3,
        out_specs=[vmem] * 5,
        compiler_params=pltpu.CompilerParams(vmem_limit_bytes=4 * 1024 * 1024),
        cost_estimate=pl.CostEstimate(flops=2_000_000, bytes_accessed=6_000_000, transcendentals=0),
        name="lay_out_kernels",
    )(kernel_one.reshape(9, 1, -1), kernel_two.reshape(9, 32, 64), kernel_three.reshape(9, 64, 128))

    vector = pl.pallas_call(
        functools.partial(score_kernel, rounds, len(blocks), order, regions, frames),
        out_shape=jax.ShapeDtypeStruct((1, LANES), F32),
        in_specs=[smem] * 3 + [vmem] * (len(blocks) + n_slab + 9) + [smem],
        out_specs=vmem,
        scratch_shapes=[
            pltpu.VMEM((regions, frames, feature_width), BF16),
            pltpu.VMEM((regions, frames, feature_width), BF16),
            pltpu.VMEM((regions * frames, frames), F32),
            pltpu.VMEM((frames, frames), F32),
            pltpu.VMEM((16 * frames, 256), BF16),
            pltpu.VMEM((17 * 64, 768), BF16),
            pltpu.VMEM((17 * 32, 768), BF16),
        ],
        compiler_params=pltpu.CompilerParams(vmem_limit_bytes=32 * 1024 * 1024),
        cost_estimate=pl.CostEstimate(flops=2_000_000_000, bytes_accessed=8_000_000, transcendentals=0),
        name="score_pair",
    )(
        candidates.T,
        query_length,
        clip_length,
        *blocks,
        *slabs,
        *weights,
        bias_one[None],
        bias_two[None],
        bias_three[None],
        kernel_four.reshape(1, -1),
        bias_four,
    )
    for k in steps:
        vector = vector + swap(vector, k)
    return vector[:, :pair_count]


def solution(mesh):
    placed = (
        P("pb", "slab", None, None),
        P(None, "pb", None, None),
        P(),
        P("pb"),
        P(),
        P(),
        P(),
        P(),
        P(),
        P(),
        P(),
        P(),
        P(),
    )
    return jax.shard_map(
        per_device, mesh=mesh, in_specs=placed, out_specs=P("pb", None), check_vma=False
    )
```

```python
import functools

import jax
import jax.numpy as jnp
from jax import lax
from jax.experimental import pallas as pl
from jax.experimental.pallas import tpu as pltpu
from jax.sharding import PartitionSpec as P

F32 = jnp.float32
BF16 = jnp.bfloat16
LANES = 128


def exchange_rounds(count):
    return list(range(count - 1, 1, -2)), list(range(count - 2, 1, -2))


def split(x):
    high = x.astype(BF16)
    return high, (x - high.astype(F32)).astype(BF16)


def split_three(x):
    high = x.astype(BF16)
    rest = x - high.astype(F32)
    middle = rest.astype(BF16)
    return high, middle, (rest - middle.astype(F32)).astype(BF16)


def pick_kernel(rounds, cand_hbm, store_ref, own_ref, *rest):
    outs, feats, cand_ref, sem = rest[:-3], rest[-3], rest[-2], rest[-1]
    query = lax.axis_index("pb")
    pair = lax.axis_index("slab")
    odd = lax.rem(pair, 2)
    steps = len(rounds[0])
    listed = pltpu.make_async_copy(cand_hbm, cand_ref, sem.at[2 * steps + 3])
    listed.start()
    copies = [pltpu.make_async_copy(own_ref, feats, sem.at[2 * steps + 2])]
    copies[0].start()
    listed.wait()
    for at, out in enumerate(outs):
        if at < steps:
            target = query ^ jnp.where(odd == 0, rounds[0][at], rounds[1][at])
            for part in range(2):
                clip = cand_ref[pair ^ part, target]
                copies.append(pltpu.make_async_copy(store_ref.at[clip], out.at[part], sem.at[2 * at + part]))
        else:
            clip = cand_ref[pair, query ^ (steps + 1 - at)]
            copies.append(pltpu.make_async_copy(store_ref.at[clip], out, sem.at[steps + at]))
    for copy in copies[1:]:
        copy.start()
    for copy in copies:
        copy.wait()


def weight_kernel(one_ref, two_ref, three_ref, w1_ref, w2_ref, w3a_ref, w3b_ref):
    row = lax.broadcasted_iota(jnp.int32, (LANES, 256), 0)
    lane = lax.broadcasted_iota(jnp.int32, (LANES, 256), 1)

    def wide(x, times):
        while times > 1:
            x = jnp.concatenate([x, x], axis=1)
            times //= 2
        return x

    def tall(x, times):
        return jnp.concatenate([x] * times, axis=0)

    group = lane // 32
    column = 2 * (group % 4) + group // 4
    slot = row // 16
    total = jnp.zeros((LANES, 256), F32)
    for d in range(3):
        for t in range(3):
            mask = (slot < 6) & (slot % 3 == d) & (row % 16 - column == t)
            total = jnp.where(mask, wide(one_ref[3 * d + t], 8), total)
    high, middle, low = split_three(total)
    both = jnp.where(slot < 3, high.astype(F32), middle.astype(F32)).astype(BF16)
    w1_ref[0:LANES, :] = both
    w1_ref[LANES : 2 * LANES, :] = both
    w1_ref[2 * LANES : 3 * LANES, :] = jnp.where(slot < 3, low.astype(F32), 0.0).astype(BF16)

    def place(ref, base, starts, value):
        for start, part in zip(starts, split_three(value)):
            for s in start:
                ref[s + base : s + base + value.shape[0], :] = part

    group = lane // 64
    column = 2 * (group % 2) + group // 2
    starts = ((0, 640), (1280,), (1920,))
    for d in range(3):
        for first, rows, base in ((0, 128, 128 * d), (4, 64, 384 + 64 * d)):
            total = jnp.zeros((rows, 256), F32)
            for t in range(3):
                tile = tall(wide(two_ref[3 * d + t], 4), rows // 32)
                total = jnp.where((row // 32 + first - column)[:rows] == t, tile, total)
            place(w2_ref, base, starts, total)
    for start in range(0, w2_ref.shape[0], 640):
        w2_ref[start + 576 : start + 640, :] = jnp.zeros((64, 256), BF16)

    column = lane // 128
    starts = ((0, 384), (768, 1152), (1536,))
    for ref, first in ((w3a_ref, 0), (w3b_ref, 2)):
        for d in range(3):
            total = jnp.zeros((LANES, 256), F32)
            for t in range(3):
                tile = tall(wide(three_ref[3 * d + t], 2), 2)
                total = jnp.where(row // 64 + first - column == t, tile, total)
            place(ref, LANES * d, starts, total)


def moved_rows(x, step):
    rows = x.shape[0]
    row = lax.broadcasted_iota(jnp.int32, x.shape, 0)
    if step == 1:
        return jnp.where(row == 0, 0.0, pltpu.roll(x, 1, 0))
    return jnp.where(row == rows - 1, 0.0, pltpu.roll(x, rows - 1, 0))


def dot(a, b):
    return jnp.dot(a, b, preferred_element_type=F32)


def score_kernel(
    rounds,
    n_blocks,
    order,
    regions,
    frames,
    cand_ref,
    qlen_ref,
    clen_ref,
    *rest,
):
    blocks = rest[:n_blocks]
    n_slabs = len(order)
    slabs = rest[n_blocks : n_blocks + n_slabs]
    (
        w1_ref,
        w2_ref,
        w3a_ref,
        w3b_ref,
        b1_ref,
        b2_ref,
        b3_ref,
        k4_ref,
        b4_ref,
        out_ref,
        clip,
        feats,
        best,
        sim,
        x1,
        x2,
        x3,
        pooled_two,
    ) = rest[n_blocks + n_slabs :]
    query = lax.axis_index("pb")
    pair = lax.axis_index("slab")
    odd = lax.rem(pair, 2)
    feature_width = feats.shape[-1]
    query_len = qlen_ref[0]
    clip_len = clen_ref[cand_ref[pair, query]]

    if n_blocks == 1:
        clip[...] = blocks[0][...]
    else:
        steps = len(rounds[0])
        band = blocks[-1].shape[1]
        pieces = [(0, blocks[-1][...]), (1, blocks[-2][...])]
        for at in range(steps):
            first, second = rounds[0][at], rounds[1][at]
            pieces.append((jnp.where(odd == 0, first, second), blocks[at][0]))
            pieces.append((jnp.where(odd == 0, second, first), blocks[steps + at][1]))
        for k, value in pieces:
            clip[:, pl.ds(pl.multiple_of((query ^ k) * band, band), band), :] = value
    for k, slab in zip(order, slabs):
        rows = slab.shape[1]
        feats[:, pl.ds(pl.multiple_of((pair ^ k) * rows, rows), rows), :] = slab[...]

    flat = feats[...].reshape(regions * frames, feature_width)
    for s in range(0, regions, 2):
        width = min(2, regions - s)
        part = clip[s : s + width].reshape(width * frames, feature_width)
        gram = lax.dot_general(flat, part, (((1,), (1,)), ((), ())), preferred_element_type=F32)
        if width == 2:
            gram = jnp.maximum(gram[:, :frames], gram[:, frames:])
        best[...] = gram if s == 0 else jnp.maximum(best[...], gram)
    total = best[0:frames, :]
    for r in range(1, regions):
        total = total + best[r * frames : (r + 1) * frames, :]
    row = lax.broadcasted_iota(jnp.int32, (frames, frames), 0)
    col = lax.broadcasted_iota(jnp.int32, (frames, frames), 1)
    sim[...] = jnp.where((row < query_len) & (col < clip_len), total * (1.0 / regions), 0.0)

    quarter = frames // 4
    phases = [sim[pl.ds(p, quarter, stride=4), :] for p in range(4)]
    ordered = jnp.concatenate([moved_rows(phases[3], 1), *phases, moved_rows(phases[0], -1)], axis=0)
    windows = frames // 8
    rolled = [pltpu.roll(ordered, 8 * m + 1, 1) for m in range(16)]
    lane = lax.broadcasted_iota(jnp.int32, (frames, LANES), 1)
    for n in range(windows):
        field = None
        for slot in range(5, -1, -1):
            d = slot % 3
            tap = rolled[(2 * slot - n) % 16][d * quarter : d * quarter + frames]
            field = tap if field is None else jnp.where(lane < 16 * slot + 16, tap, field)
        if n == 0:
            field = jnp.where(lane % 16 == 0, 0.0, field)
        if n == windows - 1:
            field = jnp.where(lane % 16 == 9, 0.0, field)
        high, low = split(field)
        x1[n * frames : (n + 1) * frames, 0:LANES] = high
        x1[n * frames : (n + 1) * frames, LANES : 2 * LANES] = low
    made = dot(x1[...], w1_ref[0:256, :]) + dot(x1[:, 0:LANES], w1_ref[256:384, :])
    made = jnp.maximum(made[:, :LANES], made[:, LANES:])
    bias_one = jnp.concatenate([b1_ref[...]] * 4, axis=1)
    bias_two = jnp.concatenate([b2_ref[...]] * 2, axis=1)
    first = []
    for n in range(windows):
        here = made[n * frames : (n + 1) * frames]
        halves = []
        for e in range(2):
            pooled = jnp.maximum(
                here[2 * e * quarter : (2 * e + 1) * quarter], here[(2 * e + 1) * quarter : (2 * e + 2) * quarter]
            )
            halves.append(jnp.maximum(pooled + bias_one, 0.0))
        first.append(halves)

    lane = lax.broadcasted_iota(jnp.int32, (quarter, LANES), 1)

    def shifted(parts, width):
        turned = [pltpu.roll(x, width, 1) for x in parts]
        result = []
        for n in range(len(parts) + 1):
            before = turned[n - 1] if n > 0 else jnp.zeros_like(turned[0])
            after = turned[n] if n < len(parts) else jnp.zeros_like(turned[0])
            result.append(jnp.where(lane < width, before, after))
        return result

    even = shifted([x[0] for x in first], 32)
    odds = shifted([x[1] for x in first], 32)
    half = 2 * quarter
    for n in range(windows + 1):
        e, o = even[n], odds[n]
        below, above = moved_rows(o, 1), moved_rows(e, -1)
        if n < windows:
            for d, values in enumerate(((below, e), (e, o), (o, above))):
                high, low = split(jnp.concatenate(values, axis=0))
                x2[n * half : (n + 1) * half, d * LANES : (d + 1) * LANES] = high
                x2[n * half : (n + 1) * half, 640 + d * LANES : 640 + (d + 1) * LANES] = low
        if n > 0:
            base = (n - 1) * half
            packed = (
                jnp.where(lane < 64, below, pltpu.roll(e, 64, 1)),
                jnp.where(lane < 64, e, pltpu.roll(o, 64, 1)),
            )
            for i, values in enumerate((packed, (o, above))):
                high, low = split(jnp.concatenate(values, axis=0))
                at = (3 + i) * LANES
                x2[base : base + half, at : at + LANES] = high
                x2[base : base + half, 640 + at : 640 + at + LANES] = low
    for n in range(0, windows, 2):
        rows = pl.ds(n * half, 2 * half)
        made = (
            dot(x2[rows, :], w2_ref[0:1280, :])
            + dot(x2[rows, 0:640], w2_ref[1280:1920, :])
            + dot(x2[rows, 0:640], w2_ref[1920:2560, :])
        )
        made = jnp.maximum(made[:, :LANES], made[:, LANES:])
        for i in range(2):
            here = jnp.maximum(made[i * half : i * half + quarter], made[i * half + quarter : (i + 1) * half])
            pooled_two[n + i] = jnp.maximum(here + bias_two, 0.0)
    second = [pooled_two[n] for n in range(windows)]

    moved = shifted(second, 64)
    for n in range(windows + 1):
        base = n * quarter
        for d, value in enumerate((moved_rows(moved[n], 1), moved[n], moved_rows(moved[n], -1))):
            high, low = split(value)
            x3[base : base + quarter, d * LANES : (d + 1) * LANES] = high
            x3[base : base + quarter, (3 + d) * LANES : (4 + d) * LANES] = low
    bias_four = b4_ref[0]
    row_best = jnp.full((quarter, 1), -2.0, F32)
    group = 4
    for n in range(0, windows, group):
        made = jnp.zeros((group * quarter, 256), F32)
        for at, ref in ((n, w3a_ref), (n + 1, w3b_ref)):
            rows = pl.ds(at * quarter, group * quarter)
            made = made + (
                dot(x3[rows, :], ref[0:768, :])
                + dot(x3[rows, :], ref[768:1536, :])
                + dot(x3[rows, 0:384], ref[1536:1920, :])
            )
        for c in range(2):
            third = jnp.maximum(made[:, c * LANES : (c + 1) * LANES] + b3_ref[...], 0.0)
            summed = jnp.sum(third * k4_ref[...], axis=1, keepdims=True)
            final = jnp.clip(summed + bias_four, -1.0, 1.0)
            for i in range(group):
                keep = 4 * (2 * (n + i) + c) < clip_len
                row_best = jnp.maximum(row_best, jnp.where(keep, final[i * quarter : (i + 1) * quarter], -2.0))
    row = lax.broadcasted_iota(jnp.int32, (quarter, 1), 0)
    kept = jnp.where(4 * row < query_len, row_best, 0.0)
    number = jnp.broadcast_to(((query_len + 3) // 4).astype(F32), (1, 1))
    score = jnp.sum(kept, axis=0, keepdims=True) / number
    lane = lax.broadcasted_iota(jnp.int32, out_ref.shape, 1)
    out_ref[...] = jnp.where(lane == pair, score, 0.0)


def per_device(
    query_feats,
    frame_store,
    candidates,
    query_length,
    clip_length,
    kernel_one,
    bias_one,
    kernel_two,
    bias_two,
    kernel_three,
    bias_three,
    kernel_four,
    bias_four,
):
    slab_rows, regions, feature_width = query_feats.shape[1:]
    band = frame_store.shape[1]
    n_query = lax.axis_size("pb")
    n_slab = lax.axis_size("slab")
    frames = band * n_query
    pair_count = candidates.shape[1]
    assert pair_count == n_slab and slab_rows * n_slab == frames == LANES
    vmem = pl.BlockSpec(memory_space=pltpu.VMEM)
    smem = pl.BlockSpec(memory_space=pltpu.SMEM)
    in_hbm = pl.BlockSpec(memory_space=pltpu.HBM)
    store = jnp.transpose(frame_store, (0, 2, 1, 3))
    own = jnp.transpose(query_feats[0], (1, 0, 2))

    def swap(x, k):
        return lax.ppermute(x, "slab", [(s, s ^ k) for s in range(n_slab)])

    rounds = None
    if n_query == 8 and n_slab % 2 == 0:
        rounds = exchange_rounds(n_query)
        steps = len(rounds[0])
        sent = pl.pallas_call(
            functools.partial(pick_kernel, rounds),
            out_shape=[jax.ShapeDtypeStruct((2, *store.shape[1:]), BF16)] * steps
            + [jax.ShapeDtypeStruct(store.shape[1:], BF16)] * 2
            + [jax.ShapeDtypeStruct(own.shape, BF16)],
            in_specs=[in_hbm] * 3,
            out_specs=[vmem] * (steps + 3),
            scratch_shapes=[
                pltpu.SMEM(candidates.T.shape, jnp.int32),
                pltpu.SemaphoreType.DMA((2 * steps + 4,)),
            ],
            compiler_params=pltpu.CompilerParams(vmem_limit_bytes=2 * 1024 * 1024),
            name="pick_bands",
        )(*[pltpu.with_memory_space_constraint(x, pltpu.HBM) for x in (candidates.T, store, own)])
        own = sent[steps + 2]
        near = []
        for at in range(steps):
            moves = [(q * n_slab + s, (q ^ rounds[s % 2][at]) * n_slab + s) for q in range(n_query) for s in range(n_slab)]
            near.append(lax.ppermute(sent[at], ("pb", "slab"), moves))
        one_away = lax.ppermute(sent[steps], "pb", [(q, q ^ 1) for q in range(n_query)])
        blocks = [*near, *[swap(x, 1) for x in near], one_away, sent[steps + 1]]
    else:
        ids = lax.dynamic_index_in_dim(candidates, lax.axis_index("slab"), 1, keepdims=False)
        got = lax.all_to_all(store[ids], "pb", 0, 0, tiled=True)
        blocks = [jnp.transpose(got, (1, 0, 2, 3)).reshape(regions, frames, feature_width)]
    slabs = [own]
    steps = [1 << i for i in range(n_slab.bit_length() - 1)]
    for k in reversed(steps):
        slabs = slabs + [swap(x, k) for x in slabs]
    order = [0]
    for k in reversed(steps):
        order = order + [o ^ k for o in order]

    weights = pl.pallas_call(
        weight_kernel,
        out_shape=[jax.ShapeDtypeStruct((rows, 256), BF16) for rows in (384, 2560, 1920, 1920)],
        in_specs=[vmem] * 3,
        out_specs=[vmem] * 4,
        compiler_params=pltpu.CompilerParams(vmem_limit_bytes=4 * 1024 * 1024),
        cost_estimate=pl.CostEstimate(flops=2_000_000, bytes_accessed=6_000_000, transcendentals=0),
        name="lay_out_kernels",
    )(kernel_one.reshape(9, 1, -1), kernel_two.reshape(9, 32, 64), kernel_three.reshape(9, 64, 128))

    vector = pl.pallas_call(
        functools.partial(score_kernel, rounds, len(blocks), order, regions, frames),
        out_shape=jax.ShapeDtypeStruct((1, LANES), F32),
        in_specs=[smem] * 3 + [vmem] * (len(blocks) + n_slab + 8) + [smem],
        out_specs=vmem,
        scratch_shapes=[
            pltpu.VMEM((regions, frames, feature_width), BF16),
            pltpu.VMEM((regions, frames, feature_width), BF16),
            pltpu.VMEM((regions * frames, frames), F32),
            pltpu.VMEM((frames, frames), F32),
            pltpu.VMEM((16 * frames, 256), BF16),
            pltpu.VMEM((16 * 64, 1280), BF16),
            pltpu.VMEM((17 * 32, 768), BF16),
            pltpu.VMEM((16, 32, LANES), F32),
        ],
        compiler_params=pltpu.CompilerParams(vmem_limit_bytes=32 * 1024 * 1024),
        cost_estimate=pl.CostEstimate(flops=2_000_000_000, bytes_accessed=8_000_000, transcendentals=0),
        name="score_pair",
    )(
        candidates.T,
        query_length,
        clip_length,
        *blocks,
        *slabs,
        *weights,
        bias_one[None],
        bias_two[None],
        bias_three[None],
        kernel_four.reshape(1, -1),
        bias_four,
    )
    vector = sum([swap(vector, k) for k in reversed(range(1, n_slab))], vector)
    return vector[:, :pair_count]


def solution(mesh):
    placed = (
        P("pb", "slab", None, None),
        P(None, "pb", None, None),
        P(),
        P("pb"),
        P(),
        P(),
        P(),
        P(),
        P(),
        P(),
        P(),
        P(),
        P(),
    )
    return jax.shard_map(
        per_device, mesh=mesh, in_specs=placed, out_specs=P("pb", None), check_vma=False
    )
```

```python
import functools

import jax
import jax.numpy as jnp
from jax import lax
from jax.experimental import pallas as pl
from jax.experimental.pallas import tpu as pltpu
from jax.sharding import PartitionSpec as P

F32 = jnp.float32
BF16 = jnp.bfloat16
LANES = 128


def exchange_rounds(count):
    return list(range(count - 1, 1, -2)), list(range(count - 2, 1, -2))


def split(x):
    high = x.astype(BF16)
    return high, (x - high.astype(F32)).astype(BF16)


def split_three(x):
    high = x.astype(BF16)
    rest = x - high.astype(F32)
    middle = rest.astype(BF16)
    return high, middle, (rest - middle.astype(F32)).astype(BF16)


def pick_kernel(rounds, cand_hbm, store_ref, own_ref, *rest):
    outs, feats, cand_ref, sem = rest[:-3], rest[-3], rest[-2], rest[-1]
    query = lax.axis_index("pb")
    pair = lax.axis_index("slab")
    odd = lax.rem(pair, 2)
    steps = len(rounds[0])
    listed = pltpu.make_async_copy(cand_hbm, cand_ref, sem.at[2 * steps + 3])
    listed.start()
    copies = [pltpu.make_async_copy(own_ref, feats, sem.at[2 * steps + 2])]
    copies[0].start()
    listed.wait()
    for at, out in enumerate(outs):
        if at < steps:
            target = query ^ jnp.where(odd == 0, rounds[0][at], rounds[1][at])
            for part in range(2):
                clip = cand_ref[pair ^ part, target]
                copies.append(pltpu.make_async_copy(store_ref.at[clip], out.at[part], sem.at[2 * at + part]))
        else:
            clip = cand_ref[pair, query ^ (steps + 1 - at)]
            copies.append(pltpu.make_async_copy(store_ref.at[clip], out, sem.at[steps + at]))
    for copy in copies[1:]:
        copy.start()
    for copy in copies:
        copy.wait()


def weight_kernel(one_ref, two_ref, three_ref, qlen_ref, b4_ref, w1_ref, w2_ref, w3a_ref, w3b_ref, qlen_out, b4_out):
    qlen_out[...] = jnp.full(qlen_out.shape, qlen_ref[0], jnp.int32)
    b4_out[...] = jnp.full(b4_out.shape, b4_ref[0], F32)
    row = lax.broadcasted_iota(jnp.int32, (LANES, 256), 0)
    lane = lax.broadcasted_iota(jnp.int32, (LANES, 256), 1)

    def wide(x, times):
        while times > 1:
            x = jnp.concatenate([x, x], axis=1)
            times //= 2
        return x

    def tall(x, times):
        return jnp.concatenate([x] * times, axis=0)

    group = lane // 32
    column = 2 * (group % 4) + group // 4
    slot = row // 16
    total = jnp.zeros((LANES, 256), F32)
    for d in range(3):
        for t in range(3):
            mask = (slot < 6) & (slot % 3 == d) & (row % 16 - column == t)
            total = jnp.where(mask, wide(one_ref[3 * d + t], 8), total)
    high, middle, low = split_three(total)
    for at, part in enumerate((middle, low)):
        both = jnp.where(slot < 3, high.astype(F32), part.astype(F32)).astype(BF16)
        w1_ref[at * LANES : (at + 1) * LANES, :] = both

    def place(ref, base, starts, value):
        for start, part in zip(starts, split_three(value)):
            for s in start:
                ref[s + base : s + base + value.shape[0], :] = part

    group = lane // 64
    column = 2 * (group % 2) + group // 2
    starts = ((0, 640), (1280,), (1920,))
    for d in range(3):
        for first, rows, base in ((0, 128, 128 * d), (4, 64, 384 + 64 * d)):
            total = jnp.zeros((rows, 256), F32)
            for t in range(3):
                tile = tall(wide(two_ref[3 * d + t], 4), rows // 32)
                total = jnp.where((row // 32 + first - column)[:rows] == t, tile, total)
            place(w2_ref, base, starts, total)
    for start in range(0, w2_ref.shape[0], 640):
        w2_ref[start + 576 : start + 640, :] = jnp.zeros((64, 256), BF16)

    column = lane // 128
    starts = ((0, 384), (768, 1152), (1536,))
    for ref, first in ((w3a_ref, 0), (w3b_ref, 2)):
        for d in range(3):
            total = jnp.zeros((LANES, 256), F32)
            for t in range(3):
                tile = tall(wide(three_ref[3 * d + t], 2), 2)
                total = jnp.where(row // 64 + first - column == t, tile, total)
            place(ref, LANES * d, starts, total)


def moved_rows(x, step):
    rows = x.shape[0]
    row = lax.broadcasted_iota(jnp.int32, x.shape, 0)
    if step == 1:
        return jnp.where(row == 0, 0.0, pltpu.roll(x, 1, 0))
    return jnp.where(row == rows - 1, 0.0, pltpu.roll(x, rows - 1, 0))


def dot(a, b):
    return jnp.dot(a, b, preferred_element_type=F32)


def score_kernel(
    rounds,
    n_blocks,
    order,
    regions,
    frames,
    cand_ref,
    qlen_ref,
    clen_ref,
    *rest,
):
    n_slabs = len(order)
    slabs, rest = rest[:n_slabs], rest[n_slabs:]
    blocks, rest = rest[:n_blocks], rest[n_blocks:]
    late = ()
    if n_blocks > 1:
        late, rest = rest[9:11], rest[:9] + rest[11:]
    (
        w1_ref,
        w2_ref,
        w3a_ref,
        w3b_ref,
        b1_ref,
        b2_ref,
        b3_ref,
        k4_ref,
        b4_ref,
        out_ref,
        clip,
        feats,
        best,
        sim,
        x1,
        x2,
        x3,
        pooled_two,
    ) = rest
    query = lax.axis_index("pb")
    pair = lax.axis_index("slab")
    odd = lax.rem(pair, 2)
    feature_width = feats.shape[-1]
    query_len = qlen_ref[...]
    clip_len = clen_ref[cand_ref[pair, query]]

    if n_blocks == 1:
        clip[...] = blocks[0][...]
    else:
        first, third, first_passed, third_passed, one_away, own = blocks
        band = own.shape[1]
        pieces = [(0, own[...]), (1, one_away[...])]
        for at, (direct, passed) in enumerate(((first, first_passed), late, (third, third_passed))):
            for value, k, other in ((direct[0], 0, 1), (passed[1], 1, 0)):
                pieces.append((jnp.where(odd == 0, rounds[k][at], rounds[other][at]), value))
        for k, value in pieces:
            clip[:, pl.ds(pl.multiple_of((query ^ k) * band, band), band), :] = value
    for k, slab in zip(order, slabs):
        rows = slab.shape[1]
        feats[:, pl.ds(pl.multiple_of((pair ^ k) * rows, rows), rows), :] = slab[...]

    flat = feats[...].reshape(regions * frames, feature_width)
    for s in range(0, regions, 2):
        width = min(2, regions - s)
        part = clip[s : s + width].reshape(width * frames, feature_width)
        gram = lax.dot_general(flat, part, (((1,), (1,)), ((), ())), preferred_element_type=F32)
        if width == 2:
            gram = jnp.maximum(gram[:, :frames], gram[:, frames:])
        best[...] = gram if s == 0 else jnp.maximum(best[...], gram)
    total = best[0:frames, :]
    for r in range(1, regions):
        total = total + best[r * frames : (r + 1) * frames, :]
    row = lax.broadcasted_iota(jnp.int32, (frames, frames), 0)
    col = lax.broadcasted_iota(jnp.int32, (frames, frames), 1)
    sim[...] = jnp.where((row < query_len) & (col < clip_len), total * (1.0 / regions), 0.0)

    quarter = frames // 4
    phases = [sim[pl.ds(p, quarter, stride=4), :] for p in range(4)]
    ordered = jnp.concatenate([moved_rows(phases[3], 1), *phases, moved_rows(phases[0], -1)], axis=0)
    windows = frames // 8
    rolled = [pltpu.roll(ordered, 8 * m + 1, 1) for m in range(16)]
    lane = lax.broadcasted_iota(jnp.int32, (frames, LANES), 1)
    for n in range(windows):
        field = None
        for slot in range(5, -1, -1):
            d = slot % 3
            tap = rolled[(2 * slot - n) % 16][d * quarter : d * quarter + frames]
            field = tap if field is None else jnp.where(lane < 16 * slot + 16, tap, field)
        if n == 0:
            field = jnp.where(lane % 16 == 0, 0.0, field)
        if n == windows - 1:
            field = jnp.where(lane % 16 == 9, 0.0, field)
        high = field.astype(BF16)
        low = jnp.where(lane < 48, field - high.astype(F32), field).astype(BF16)
        x1[n * frames : (n + 1) * frames, 0:LANES] = high
        x1[n * frames : (n + 1) * frames, LANES : 2 * LANES] = low
    made = dot(x1[...], w1_ref[...])
    made = jnp.maximum(made[:, :LANES], made[:, LANES:])
    bias_one = jnp.concatenate([b1_ref[...]] * 4, axis=1)
    bias_two = jnp.concatenate([b2_ref[...]] * 2, axis=1)
    first = []
    for n in range(windows):
        here = made[n * frames : (n + 1) * frames]
        halves = []
        for e in range(2):
            pooled = jnp.maximum(
                here[2 * e * quarter : (2 * e + 1) * quarter], here[(2 * e + 1) * quarter : (2 * e + 2) * quarter]
            )
            halves.append(jnp.maximum(pooled + bias_one, 0.0))
        first.append(halves)

    lane = lax.broadcasted_iota(jnp.int32, (quarter, LANES), 1)

    def shifted(parts, width):
        turned = [pltpu.roll(x, width, 1) for x in parts]
        result = []
        for n in range(len(parts) + 1):
            before = turned[n - 1] if n > 0 else jnp.zeros_like(turned[0])
            after = turned[n] if n < len(parts) else jnp.zeros_like(turned[0])
            result.append(jnp.where(lane < width, before, after))
        return result

    even = shifted([x[0] for x in first], 32)
    odds = shifted([x[1] for x in first], 32)
    half = 2 * quarter
    for n in range(windows + 1):
        e, o = even[n], odds[n]
        below, above = moved_rows(o, 1), moved_rows(e, -1)
        if n < windows:
            for d, values in enumerate(((below, e), (e, o), (o, above))):
                high, low = split(jnp.concatenate(values, axis=0))
                x2[n * half : (n + 1) * half, d * LANES : (d + 1) * LANES] = high
                x2[n * half : (n + 1) * half, 640 + d * LANES : 640 + (d + 1) * LANES] = low
        if n > 0:
            base = (n - 1) * half
            packed = (
                jnp.where(lane < 64, below, pltpu.roll(e, 64, 1)),
                jnp.where(lane < 64, e, pltpu.roll(o, 64, 1)),
            )
            for i, values in enumerate((packed, (o, above))):
                high, low = split(jnp.concatenate(values, axis=0))
                at = (3 + i) * LANES
                x2[base : base + half, at : at + LANES] = high
                x2[base : base + half, 640 + at : 640 + at + LANES] = low
    for n in range(0, windows, 2):
        rows = pl.ds(n * half, 2 * half)
        made = (
            dot(x2[rows, :], w2_ref[0:1280, :])
            + dot(x2[rows, 0:640], w2_ref[1280:1920, :])
            + dot(x2[rows, 0:640], w2_ref[1920:2560, :])
        )
        made = jnp.maximum(made[:, :LANES], made[:, LANES:])
        for i in range(2):
            here = jnp.maximum(made[i * half : i * half + quarter], made[i * half + quarter : (i + 1) * half])
            pooled_two[n + i] = jnp.maximum(here + bias_two, 0.0)
    second = [pooled_two[n] for n in range(windows)]

    moved = shifted(second, 64)
    for n in range(windows + 1):
        base = n * quarter
        for d, value in enumerate((moved_rows(moved[n], 1), moved[n], moved_rows(moved[n], -1))):
            high, low = split(value)
            x3[base : base + quarter, d * LANES : (d + 1) * LANES] = high
            x3[base : base + quarter, (3 + d) * LANES : (4 + d) * LANES] = low
    bias_four = b4_ref[...]
    row_best = jnp.full((quarter, LANES), -2.0, F32)
    group = 4
    for n in range(0, windows, group):
        made = jnp.zeros((group * quarter, 256), F32)
        for at, ref in ((n, w3a_ref), (n + 1, w3b_ref)):
            rows = pl.ds(at * quarter, group * quarter)
            made = made + (
                dot(x3[rows, :], ref[0:768, :])
                + dot(x3[rows, :], ref[768:1536, :])
                + dot(x3[rows, 0:384], ref[1536:1920, :])
            )
        for c in range(2):
            third = jnp.maximum(made[:, c * LANES : (c + 1) * LANES] + b3_ref[...], 0.0)
            summed = jnp.sum(third * k4_ref[...], axis=1, keepdims=True)
            final = jnp.clip(summed + bias_four, -1.0, 1.0)
            for i in range(group):
                keep = 4 * (2 * (n + i) + c) < clip_len
                row_best = jnp.maximum(row_best, jnp.where(keep, final[i * quarter : (i + 1) * quarter], -2.0))
    row = lax.broadcasted_iota(jnp.int32, (quarter, LANES), 0)
    kept = jnp.where(4 * row < query_len, row_best, 0.0)
    score = jnp.sum(kept, axis=0, keepdims=True) / ((query_len + 3) // 4).astype(F32)
    lane = lax.broadcasted_iota(jnp.int32, out_ref.shape, 1)
    out_ref[...] = jnp.where(lane == pair, score, 0.0)


def per_device(
    query_feats,
    frame_store,
    candidates,
    query_length,
    clip_length,
    kernel_one,
    bias_one,
    kernel_two,
    bias_two,
    kernel_three,
    bias_three,
    kernel_four,
    bias_four,
):
    slab_rows, regions, feature_width = query_feats.shape[1:]
    band = frame_store.shape[1]
    n_query = lax.axis_size("pb")
    n_slab = lax.axis_size("slab")
    frames = band * n_query
    pair_count = candidates.shape[1]
    assert pair_count == n_slab and slab_rows * n_slab == frames == LANES
    vmem = pl.BlockSpec(memory_space=pltpu.VMEM)
    smem = pl.BlockSpec(memory_space=pltpu.SMEM)
    in_hbm = pl.BlockSpec(memory_space=pltpu.HBM)
    store = jnp.transpose(frame_store, (0, 2, 1, 3))
    own = jnp.transpose(query_feats[0], (1, 0, 2))

    def swap(x, k):
        return lax.ppermute(x, "slab", [(s, s ^ k) for s in range(n_slab)])

    rounds = None
    if n_query == 8 and n_slab % 2 == 0:
        rounds = exchange_rounds(n_query)
        steps = len(rounds[0])
        sent = pl.pallas_call(
            functools.partial(pick_kernel, rounds),
            out_shape=[jax.ShapeDtypeStruct((2, *store.shape[1:]), BF16)] * steps
            + [jax.ShapeDtypeStruct(store.shape[1:], BF16)] * 2
            + [jax.ShapeDtypeStruct(own.shape, BF16)],
            in_specs=[in_hbm] * 3,
            out_specs=[vmem] * (steps + 3),
            scratch_shapes=[
                pltpu.SMEM(candidates.T.shape, jnp.int32),
                pltpu.SemaphoreType.DMA((2 * steps + 4,)),
            ],
            compiler_params=pltpu.CompilerParams(vmem_limit_bytes=2 * 1024 * 1024),
            name="pick_bands",
        )(*[pltpu.with_memory_space_constraint(x, pltpu.HBM) for x in (candidates.T, store, own)])
        def cross(at):
            moves = [(q * n_slab + s, (q ^ rounds[s % 2][at]) * n_slab + s) for q in range(n_query) for s in range(n_slab)]
            return lax.ppermute(sent[at], ("pb", "slab"), moves)

        first, third = cross(0), cross(2)
        own = sent[steps + 2]
    else:
        ids = lax.dynamic_index_in_dim(candidates, lax.axis_index("slab"), 1, keepdims=False)
        got = lax.all_to_all(store[ids], "pb", 0, 0, tiled=True)
        blocks = [jnp.transpose(got, (1, 0, 2, 3)).reshape(regions, frames, feature_width)]
    slabs = [own]
    hops = [1 << i for i in range(n_slab.bit_length() - 1)]
    for k in reversed(hops):
        slabs = slabs + [swap(x, k) for x in slabs]
    order = [0]
    for k in reversed(hops):
        order = order + [o ^ k for o in order]
    if rounds is not None:
        one_away = lax.ppermute(sent[steps], "pb", [(q, q ^ 1) for q in range(n_query)])
        blocks = [first, third, swap(first, 1), swap(third, 1), one_away, sent[steps + 1]]

    weights = pl.pallas_call(
        weight_kernel,
        out_shape=[jax.ShapeDtypeStruct((rows, 256), BF16) for rows in (256, 2560, 1920, 1920)]
        + [jax.ShapeDtypeStruct((1, LANES), t) for t in (jnp.int32, F32)],
        in_specs=[vmem] * 3 + [smem] * 2,
        out_specs=[vmem] * 6,
        compiler_params=pltpu.CompilerParams(vmem_limit_bytes=10 * 1024 * 1024),
        cost_estimate=pl.CostEstimate(flops=2_000_000, bytes_accessed=6_000_000, transcendentals=0),
        name="lay_out_kernels",
    )(
        kernel_one.reshape(9, 1, -1),
        kernel_two.reshape(9, 32, 64),
        kernel_three.reshape(9, 64, 128),
        query_length,
        bias_four,
    )
    *weights, query_len, last_bias = weights
    late = []
    if rounds is not None:
        second = cross(1)
        second, weights[0] = lax.optimization_barrier((second, weights[0]))
        late = [second, swap(second, 1)]

    vector = pl.pallas_call(
        functools.partial(score_kernel, rounds, len(blocks), order, regions, frames),
        out_shape=jax.ShapeDtypeStruct((1, LANES), F32),
        in_specs=[smem, vmem, smem] + [vmem] * (len(blocks) + len(late) + n_slab + 9),
        out_specs=vmem,
        scratch_shapes=[
            pltpu.VMEM((regions, frames, feature_width), BF16),
            pltpu.VMEM((regions, frames, feature_width), BF16),
            pltpu.VMEM((regions * frames, frames), F32),
            pltpu.VMEM((frames, frames), F32),
            pltpu.VMEM((16 * frames, 256), BF16),
            pltpu.VMEM((16 * 64, 1280), BF16),
            pltpu.VMEM((17 * 32, 768), BF16),
            pltpu.VMEM((16, 32, LANES), F32),
        ],
        compiler_params=pltpu.CompilerParams(vmem_limit_bytes=32 * 1024 * 1024),
        cost_estimate=pl.CostEstimate(flops=2_000_000_000, bytes_accessed=8_000_000, transcendentals=0),
        name="score_pair",
    )(
        candidates.T,
        query_len,
        clip_length,
        *slabs,
        *blocks,
        *weights,
        bias_one[None],
        bias_two[None],
        bias_three[None],
        kernel_four.reshape(1, -1),
        last_bias,
        *late,
    )
    vector = sum([swap(vector, k) for k in reversed(range(1, n_slab))], vector)
    return vector[:, :pair_count]


def solution(mesh):
    placed = (
        P("pb", "slab", None, None),
        P(None, "pb", None, None),
        P(),
        P("pb"),
        P(),
        P(),
        P(),
        P(),
        P(),
        P(),
        P(),
        P(),
        P(),
    )
    return jax.shard_map(
        per_device, mesh=mesh, in_specs=placed, out_specs=P("pb", None), check_vma=False
    )
```

```python
import functools

import jax
import jax.numpy as jnp
from jax import lax
from jax.experimental import pallas as pl
from jax.experimental.pallas import tpu as pltpu
from jax.sharding import PartitionSpec as P

F32 = jnp.float32
BF16 = jnp.bfloat16
LANES = 128


def exchange_rounds(count):
    odd, even = list(range(count - 1, 1, -2)), list(range(count - 2, 1, -2))
    return odd, [even[1], even[0], *even[2:]]


def split(x):
    high = x.astype(BF16)
    return high, (x - high.astype(F32)).astype(BF16)


def split_three(x):
    high = x.astype(BF16)
    rest = x - high.astype(F32)
    middle = rest.astype(BF16)
    return high, middle, (rest - middle.astype(F32)).astype(BF16)


def pick_kernel(rounds, cand_hbm, store_ref, own_ref, *rest):
    outs, feats, cand_ref, sem = rest[:-3], rest[-3], rest[-2], rest[-1]
    query = lax.axis_index("pb")
    pair = lax.axis_index("slab")
    odd = lax.rem(pair, 2)
    steps = len(rounds[0])
    listed = pltpu.make_async_copy(cand_hbm, cand_ref, sem.at[2 * steps + 3])
    listed.start()
    copies = [pltpu.make_async_copy(own_ref, feats, sem.at[2 * steps + 2])]
    copies[0].start()
    listed.wait()
    for at, out in enumerate(outs):
        if at < steps:
            target = query ^ jnp.where(odd == 0, rounds[0][at], rounds[1][at])
            for part in range(2):
                clip = cand_ref[pair ^ part, target]
                copies.append(pltpu.make_async_copy(store_ref.at[clip], out.at[part], sem.at[2 * at + part]))
        else:
            clip = cand_ref[pair, query ^ (steps + 1 - at)]
            copies.append(pltpu.make_async_copy(store_ref.at[clip], out, sem.at[steps + at]))
    for copy in copies[1:]:
        copy.start()
    for copy in copies:
        copy.wait()


def weight_kernel(one_ref, two_ref, three_ref, qlen_ref, b4_ref, w1_ref, w2_ref, w3_ref, qlen_out, b4_out):
    qlen_out[...] = jnp.full(qlen_out.shape, qlen_ref[0], jnp.int32)
    b4_out[...] = jnp.full(b4_out.shape, b4_ref[0], F32)
    row = lax.broadcasted_iota(jnp.int32, (LANES, 256), 0)
    lane = lax.broadcasted_iota(jnp.int32, (LANES, 256), 1)

    def wide(x, times):
        while times > 1:
            x = jnp.concatenate([x, x], axis=1)
            times //= 2
        return x

    def tall(x, times):
        return jnp.concatenate([x] * times, axis=0)

    group = lane // 32
    column = 2 * (group % 4) + group // 4
    slot = row // 16
    total = jnp.zeros((LANES, 256), F32)
    for d in range(3):
        for t in range(3):
            mask = (slot < 6) & (slot % 3 == d) & (row % 16 - column == t)
            total = jnp.where(mask, wide(one_ref[3 * d + t], 8), total)
    high, middle, low = split_three(total)
    for at, part in enumerate((middle, low)):
        both = jnp.where(slot < 3, high.astype(F32), part.astype(F32)).astype(BF16)
        w1_ref[at * LANES : (at + 1) * LANES, :] = both

    def place(ref, base, starts, value):
        for start, part in zip(starts, split_three(value)):
            for s in start:
                ref[s + base : s + base + value.shape[0], :] = part

    group = lane // 64
    column = 2 * (group % 2) + group // 2
    starts = ((0, 640), (1280,), (1920,))
    for d in range(3):
        for first, rows, base in ((0, 128, 128 * d), (4, 64, 384 + 64 * d)):
            total = jnp.zeros((rows, 256), F32)
            for t in range(3):
                tile = tall(wide(two_ref[3 * d + t], 4), rows // 32)
                total = jnp.where((row // 32 + first - column)[:rows] == t, tile, total)
            place(w2_ref, base, starts, total)
    for start in range(0, w2_ref.shape[0], 640):
        w2_ref[start + 576 : start + 640, :] = jnp.zeros((64, 256), BF16)

    column = lane // 128
    for at, first in ((0, 0), (1, 2)):
        for d in range(3):
            total = jnp.zeros((LANES, 256), F32)
            for t in range(3):
                tile = tall(wide(three_ref[3 * d + t], 2), 2)
                total = jnp.where(row // 64 + first - column == t, tile, total)
            place(w3_ref, LANES * d, ((768 * at, 768 * at + 384), (1536 + 384 * at,)), total)


def moved_rows(x, step):
    rows = x.shape[0]
    row = lax.broadcasted_iota(jnp.int32, x.shape, 0)
    if step == 1:
        return jnp.where(row == 0, 0.0, pltpu.roll(x, 1, 0))
    return jnp.where(row == rows - 1, 0.0, pltpu.roll(x, rows - 1, 0))


def dot(a, b):
    return jnp.dot(a, b, preferred_element_type=F32)


def score_kernel(
    rounds,
    n_blocks,
    order,
    regions,
    frames,
    cand_ref,
    qlen_ref,
    clen_ref,
    *rest,
):
    n_slabs = len(order)
    slabs, rest = rest[:n_slabs], rest[n_slabs:]
    blocks, rest = rest[:n_blocks], rest[n_blocks:]
    late = ()
    if n_blocks > 1:
        late, rest = rest[8:10], rest[:8] + rest[10:]
    (
        w1_ref,
        w2_ref,
        w3_ref,
        b1_ref,
        b2_ref,
        b3_ref,
        k4_ref,
        b4_ref,
        out_ref,
        clip,
        feats,
        best,
        sim,
        x1,
        x2,
        x3,
        pooled_two,
    ) = rest
    query = lax.axis_index("pb")
    pair = lax.axis_index("slab")
    odd = lax.rem(pair, 2)
    feature_width = feats.shape[-1]
    query_len = qlen_ref[...]
    clip_len = clen_ref[cand_ref[pair, query]]

    if n_blocks == 1:
        clip[...] = blocks[0][...]
    else:
        third, first, third_passed, first_passed, one_away, own = blocks
        band = own.shape[1]
        pieces = [(0, own[...]), (1, one_away[...])]
        for at, (direct, passed) in enumerate(((first, first_passed), late, (third, third_passed))):
            for value, k, other in ((direct[0], 0, 1), (passed[1], 1, 0)):
                pieces.append((jnp.where(odd == 0, rounds[k][at], rounds[other][at]), value))
        for k, value in pieces:
            clip[:, pl.ds(pl.multiple_of((query ^ k) * band, band), band), :] = value
    for k, slab in zip(order, slabs):
        rows = slab.shape[1]
        feats[:, pl.ds(pl.multiple_of((pair ^ k) * rows, rows), rows), :] = slab[...]

    flat = feats[...].reshape(regions * frames, feature_width)
    for s in range(0, regions, 2):
        width = min(2, regions - s)
        part = clip[s : s + width].reshape(width * frames, feature_width)
        gram = lax.dot_general(flat, part, (((1,), (1,)), ((), ())), preferred_element_type=F32)
        if width == 2:
            gram = jnp.maximum(gram[:, :frames], gram[:, frames:])
        best[...] = gram if s == 0 else jnp.maximum(best[...], gram)
    total = best[0:frames, :]
    for r in range(1, regions):
        total = total + best[r * frames : (r + 1) * frames, :]
    row = lax.broadcasted_iota(jnp.int32, (frames, frames), 0)
    col = lax.broadcasted_iota(jnp.int32, (frames, frames), 1)
    sim[...] = jnp.where((row < query_len) & (col < clip_len), total * (1.0 / regions), 0.0)

    quarter = frames // 4
    phases = [sim[pl.ds(p, quarter, stride=4), :] for p in range(4)]
    ordered = jnp.concatenate([moved_rows(phases[3], 1), *phases, moved_rows(phases[0], -1)], axis=0)
    windows = frames // 8
    rolled = [pltpu.roll(ordered, 8 * m + 1, 1) for m in range(16)]
    lane = lax.broadcasted_iota(jnp.int32, (frames, LANES), 1)
    for n in range(windows):
        field = None
        for slot in range(5, -1, -1):
            d = slot % 3
            tap = rolled[(2 * slot - n) % 16][d * quarter : d * quarter + frames]
            field = tap if field is None else jnp.where(lane < 16 * slot + 16, tap, field)
        if n == 0:
            field = jnp.where(lane % 16 == 0, 0.0, field)
        if n == windows - 1:
            field = jnp.where(lane % 16 == 9, 0.0, field)
        high = field.astype(BF16)
        low = jnp.where(lane < 48, field - high.astype(F32), field).astype(BF16)
        x1[n * frames : (n + 1) * frames, 0:LANES] = high
        x1[n * frames : (n + 1) * frames, LANES : 2 * LANES] = low
    made = dot(x1[...], w1_ref[...])
    made = jnp.maximum(made[:, :LANES], made[:, LANES:])
    bias_one = jnp.concatenate([b1_ref[...]] * 4, axis=1)
    bias_two = jnp.concatenate([b2_ref[...]] * 2, axis=1)
    first = []
    for n in range(windows):
        here = made[n * frames : (n + 1) * frames]
        halves = []
        for e in range(2):
            pooled = jnp.maximum(
                here[2 * e * quarter : (2 * e + 1) * quarter], here[(2 * e + 1) * quarter : (2 * e + 2) * quarter]
            )
            halves.append(jnp.maximum(pooled + bias_one, 0.0))
        first.append(halves)

    lane = lax.broadcasted_iota(jnp.int32, (quarter, LANES), 1)

    def shifted(parts, width):
        turned = [pltpu.roll(x, width, 1) for x in parts]
        result = []
        for n in range(len(parts) + 1):
            before = turned[n - 1] if n > 0 else jnp.zeros_like(turned[0])
            after = turned[n] if n < len(parts) else jnp.zeros_like(turned[0])
            result.append(jnp.where(lane < width, before, after))
        return result

    even = shifted([x[0] for x in first], 32)
    odds = shifted([x[1] for x in first], 32)
    half = 2 * quarter
    for n in range(windows + 1):
        e, o = even[n], odds[n]
        below, above = moved_rows(o, 1), moved_rows(e, -1)
        if n < windows:
            for d, values in enumerate(((below, e), (e, o), (o, above))):
                high, low = split(jnp.concatenate(values, axis=0))
                x2[n * half : (n + 1) * half, d * LANES : (d + 1) * LANES] = high
                x2[n * half : (n + 1) * half, 640 + d * LANES : 640 + (d + 1) * LANES] = low
        if n > 0:
            base = (n - 1) * half
            packed = (
                jnp.where(lane < 64, below, pltpu.roll(e, 64, 1)),
                jnp.where(lane < 64, e, pltpu.roll(o, 64, 1)),
            )
            for i, values in enumerate((packed, (o, above))):
                high, low = split(jnp.concatenate(values, axis=0))
                at = (3 + i) * LANES
                x2[base : base + half, at : at + LANES] = high
                x2[base : base + half, 640 + at : 640 + at + LANES] = low
    for n in range(0, windows, 2):
        left = x2[n * half : (n + 2) * half, :]
        made = dot(jnp.concatenate([left, left[:, :640], left[:, :640]], axis=1), w2_ref[...])
        made = jnp.maximum(made[:, :LANES], made[:, LANES:])
        for i in range(2):
            here = jnp.maximum(made[i * half : i * half + quarter], made[i * half + quarter : (i + 1) * half])
            pooled_two[n + i] = jnp.maximum(here + bias_two, 0.0)
    second = [pooled_two[n] for n in range(windows)]

    moved = shifted(second, 64)
    for n in range(windows + 1):
        base = n * quarter
        for d, value in enumerate((moved_rows(moved[n], 1), moved[n], moved_rows(moved[n], -1))):
            high, low = split(value)
            x3[base : base + quarter, d * LANES : (d + 1) * LANES] = high
            x3[base : base + quarter, (3 + d) * LANES : (4 + d) * LANES] = low
    bias_four = b4_ref[...]
    row_best = jnp.full((quarter, LANES), -2.0, F32)
    group = 4
    for n in range(0, windows, group):
        left = x3[n * quarter : (n + group) * quarter, :]
        right = x3[(n + 1) * quarter : (n + 1 + group) * quarter, :]
        made = dot(jnp.concatenate([left, right, left[:, :384], right[:, :384]], axis=1), w3_ref[...])
        for c in range(2):
            third = jnp.maximum(made[:, c * LANES : (c + 1) * LANES] + b3_ref[...], 0.0)
            summed = jnp.sum(third * k4_ref[...], axis=1, keepdims=True)
            final = jnp.clip(summed + bias_four, -1.0, 1.0)
            for i in range(group):
                keep = 4 * (2 * (n + i) + c) < clip_len
                row_best = jnp.maximum(row_best, jnp.where(keep, final[i * quarter : (i + 1) * quarter], -2.0))
    row = lax.broadcasted_iota(jnp.int32, (quarter, LANES), 0)
    kept = jnp.where(4 * row < query_len, row_best, 0.0)
    score = jnp.sum(kept, axis=0, keepdims=True) / ((query_len + 3) // 4).astype(F32)
    lane = lax.broadcasted_iota(jnp.int32, out_ref.shape, 1)
    out_ref[...] = jnp.where(lane == pair, score, 0.0)


def per_device(
    query_feats,
    frame_store,
    candidates,
    query_length,
    clip_length,
    kernel_one,
    bias_one,
    kernel_two,
    bias_two,
    kernel_three,
    bias_three,
    kernel_four,
    bias_four,
):
    slab_rows, regions, feature_width = query_feats.shape[1:]
    band = frame_store.shape[1]
    n_query = lax.axis_size("pb")
    n_slab = lax.axis_size("slab")
    frames = band * n_query
    pair_count = candidates.shape[1]
    assert pair_count == n_slab and slab_rows * n_slab == frames == LANES
    vmem = pl.BlockSpec(memory_space=pltpu.VMEM)
    smem = pl.BlockSpec(memory_space=pltpu.SMEM)
    in_hbm = pl.BlockSpec(memory_space=pltpu.HBM)
    store = jnp.transpose(frame_store, (0, 2, 1, 3))
    own = jnp.transpose(query_feats[0], (1, 0, 2))

    def swap(x, k):
        return lax.ppermute(x, "slab", [(s, s ^ k) for s in range(n_slab)])

    rounds = None
    if n_query == 8 and n_slab % 2 == 0:
        rounds = exchange_rounds(n_query)
        steps = len(rounds[0])
        sent = pl.pallas_call(
            functools.partial(pick_kernel, rounds),
            out_shape=[jax.ShapeDtypeStruct((2, *store.shape[1:]), BF16)] * steps
            + [jax.ShapeDtypeStruct(store.shape[1:], BF16)] * 2
            + [jax.ShapeDtypeStruct(own.shape, BF16)],
            in_specs=[in_hbm] * 3,
            out_specs=[vmem] * (steps + 3),
            scratch_shapes=[
                pltpu.SMEM(candidates.T.shape, jnp.int32),
                pltpu.SemaphoreType.DMA((2 * steps + 4,)),
            ],
            compiler_params=pltpu.CompilerParams(vmem_limit_bytes=2 * 1024 * 1024),
            name="pick_bands",
        )(*[pltpu.with_memory_space_constraint(x, pltpu.HBM) for x in (candidates.T, store, own)])
        def cross(at):
            moves = [(q * n_slab + s, (q ^ rounds[s % 2][at]) * n_slab + s) for q in range(n_query) for s in range(n_slab)]
            return lax.ppermute(sent[at], ("pb", "slab"), moves)

        third, first = cross(2), cross(0)
        own = sent[steps + 2]
    else:
        ids = lax.dynamic_index_in_dim(candidates, lax.axis_index("slab"), 1, keepdims=False)
        got = lax.all_to_all(store[ids], "pb", 0, 0, tiled=True)
        blocks = [jnp.transpose(got, (1, 0, 2, 3)).reshape(regions, frames, feature_width)]
    slabs = [own]
    hops = [1 << i for i in range(n_slab.bit_length() - 1)]
    for k in reversed(hops):
        slabs = slabs + [swap(x, k) for x in slabs]
    order = [0]
    for k in reversed(hops):
        order = order + [o ^ k for o in order]
    if rounds is not None:
        one_away = lax.ppermute(sent[steps], "pb", [(q, q ^ 1) for q in range(n_query)])
        blocks = [third, first, swap(third, 1), swap(first, 1), one_away, sent[steps + 1]]

    weights = pl.pallas_call(
        weight_kernel,
        out_shape=[jax.ShapeDtypeStruct((rows, 256), BF16) for rows in (256, 2560, 2304)]
        + [jax.ShapeDtypeStruct((1, LANES), t) for t in (jnp.int32, F32)],
        in_specs=[vmem] * 3 + [smem] * 2,
        out_specs=[vmem] * 5,
        compiler_params=pltpu.CompilerParams(vmem_limit_bytes=10 * 1024 * 1024),
        cost_estimate=pl.CostEstimate(flops=2_000_000, bytes_accessed=6_000_000, transcendentals=0),
        name="lay_out_kernels",
    )(
        kernel_one.reshape(9, 1, -1),
        kernel_two.reshape(9, 32, 64),
        kernel_three.reshape(9, 64, 128),
        query_length,
        bias_four,
    )
    *weights, query_len, last_bias = weights
    late = []
    if rounds is not None:
        second = cross(1)
        second, weights[0] = lax.optimization_barrier((second, weights[0]))
        late = [second, swap(second, 1)]

    vector = pl.pallas_call(
        functools.partial(score_kernel, rounds, len(blocks), order, regions, frames),
        out_shape=jax.ShapeDtypeStruct((1, LANES), F32),
        in_specs=[smem, vmem, smem] + [vmem] * (len(blocks) + len(late) + n_slab + 8),
        out_specs=vmem,
        scratch_shapes=[
            pltpu.VMEM((regions, frames, feature_width), BF16),
            pltpu.VMEM((regions, frames, feature_width), BF16),
            pltpu.VMEM((regions * frames, frames), F32),
            pltpu.VMEM((frames, frames), F32),
            pltpu.VMEM((16 * frames, 256), BF16),
            pltpu.VMEM((16 * 64, 1280), BF16),
            pltpu.VMEM((17 * 32, 768), BF16),
            pltpu.VMEM((16, 32, LANES), F32),
        ],
        compiler_params=pltpu.CompilerParams(vmem_limit_bytes=32 * 1024 * 1024),
        cost_estimate=pl.CostEstimate(flops=2_000_000_000, bytes_accessed=8_000_000, transcendentals=0),
        name="score_pair",
    )(
        candidates.T,
        query_len,
        clip_length,
        *slabs,
        *blocks,
        *weights,
        bias_one[None],
        bias_two[None],
        bias_three[None],
        kernel_four.reshape(1, -1),
        last_bias,
        *late,
    )
    vector = sum([swap(vector, k) for k in reversed(range(1, n_slab))], vector)
    return vector[:, :pair_count]


def solution(mesh):
    placed = (
        P("pb", "slab", None, None),
        P(None, "pb", None, None),
        P(),
        P("pb"),
        P(),
        P(),
        P(),
        P(),
        P(),
        P(),
        P(),
        P(),
        P(),
    )
    return jax.shard_map(
        per_device, mesh=mesh, in_specs=placed, out_specs=P("pb", None), check_vma=False
    )
```

```python
import functools

import jax
import jax.numpy as jnp
from jax import lax
from jax.experimental import pallas as pl
from jax.experimental.pallas import tpu as pltpu
from jax.sharding import PartitionSpec as P

F32 = jnp.float32
BF16 = jnp.bfloat16
LANES = 128


def exchange_rounds(count):
    odd, even = list(range(count - 1, 1, -2)), list(range(count - 2, 1, -2))
    return odd, [even[1], even[0], *even[2:]]


def split(x):
    high = x.astype(BF16)
    return high, (x - high.astype(F32)).astype(BF16)


def split_three(x):
    high = x.astype(BF16)
    rest = x - high.astype(F32)
    middle = rest.astype(BF16)
    return high, middle, (rest - middle.astype(F32)).astype(BF16)


def pick_kernel(rounds, cand_hbm, store_ref, own_ref, *rest):
    outs, feats, cand_ref, sem = rest[:-3], rest[-3], rest[-2], rest[-1]
    query = lax.axis_index("pb")
    pair = lax.axis_index("slab")
    odd = lax.rem(pair, 2)
    steps = len(rounds[0])
    listed = pltpu.make_async_copy(cand_hbm, cand_ref, sem.at[2 * steps + 3])
    listed.start()
    copies = [pltpu.make_async_copy(own_ref, feats, sem.at[2 * steps + 2])]
    copies[0].start()
    listed.wait()
    for at, out in enumerate(outs):
        if at < steps:
            target = query ^ jnp.where(odd == 0, rounds[0][at], rounds[1][at])
            for part in range(2):
                clip = cand_ref[pair ^ part, target]
                copies.append(pltpu.make_async_copy(store_ref.at[clip], out.at[part], sem.at[2 * at + part]))
        else:
            clip = cand_ref[pair, query ^ (steps + 1 - at)]
            copies.append(pltpu.make_async_copy(store_ref.at[clip], out, sem.at[steps + at]))
    for copy in copies[1:]:
        copy.start()
    for copy in copies:
        copy.wait()


def weight_kernel(
    one_ref,
    two_ref,
    three_ref,
    cand_ref,
    qlen_ref,
    clen_ref,
    b4_ref,
    w1_ref,
    w2_ref,
    w3_ref,
    qlen_out,
    clen_out,
    b4_out,
):
    qlen_out[...] = jnp.full(qlen_out.shape, qlen_ref[0], jnp.int32)
    clip_len = clen_ref[cand_ref[lax.axis_index("slab"), lax.axis_index("pb")]]
    clen_out[...] = jnp.full(clen_out.shape, clip_len, jnp.int32)
    b4_out[...] = jnp.full(b4_out.shape, b4_ref[0], F32)
    row = lax.broadcasted_iota(jnp.int32, (LANES, 256), 0)
    lane = lax.broadcasted_iota(jnp.int32, (LANES, 256), 1)

    def wide(x, times):
        while times > 1:
            x = jnp.concatenate([x, x], axis=1)
            times //= 2
        return x

    def tall(x, times):
        return jnp.concatenate([x] * times, axis=0)

    group = lane // 32
    column = 2 * (group % 4) + group // 4
    slot = row // 16
    total = jnp.zeros((LANES, 256), F32)
    for d in range(3):
        for t in range(3):
            mask = (slot < 6) & (slot % 3 == d) & (row % 16 - column == t)
            total = jnp.where(mask, wide(one_ref[3 * d + t], 8), total)
    high, middle, low = split_three(total)
    for at, part in enumerate((middle, low)):
        both = jnp.where(slot < 3, high.astype(F32), part.astype(F32)).astype(BF16)
        w1_ref[at * LANES : (at + 1) * LANES, :] = both

    def place(ref, base, starts, value):
        for start, part in zip(starts, split_three(value)):
            for s in start:
                ref[s + base : s + base + value.shape[0], :] = part

    group = lane // 64
    column = 2 * (group % 2) + group // 2
    starts = ((0, 640), (1280,), (1920,))
    for d in range(3):
        for first, rows, base in ((0, 128, 128 * d), (4, 64, 384 + 64 * d)):
            total = jnp.zeros((rows, 256), F32)
            for t in range(3):
                tile = tall(wide(two_ref[3 * d + t], 4), rows // 32)
                total = jnp.where((row // 32 + first - column)[:rows] == t, tile, total)
            place(w2_ref, base, starts, total)
    for start in range(0, w2_ref.shape[0], 640):
        w2_ref[start + 576 : start + 640, :] = jnp.zeros((64, 256), BF16)

    column = lane // 128
    for at, first in ((0, 0), (1, 2)):
        for d in range(3):
            total = jnp.zeros((LANES, 256), F32)
            for t in range(3):
                tile = tall(wide(three_ref[3 * d + t], 2), 2)
                total = jnp.where(row // 64 + first - column == t, tile, total)
            place(w3_ref, LANES * d, ((768 * at, 768 * at + 384), (1536 + 384 * at,)), total)


def moved_rows(x, step):
    rows = x.shape[0]
    row = lax.broadcasted_iota(jnp.int32, x.shape, 0)
    if step == 1:
        return jnp.where(row == 0, 0.0, pltpu.roll(x, 1, 0))
    return jnp.where(row == rows - 1, 0.0, pltpu.roll(x, rows - 1, 0))


def dot(a, b):
    return jnp.dot(a, b, preferred_element_type=F32)


def score_kernel(
    rounds,
    n_blocks,
    order,
    regions,
    frames,
    qlen_ref,
    clen_ref,
    *rest,
):
    n_slabs = len(order)
    slabs, rest = rest[:n_slabs], rest[n_slabs:]
    blocks, rest = rest[:n_blocks], rest[n_blocks:]
    late = ()
    if n_blocks > 1:
        late, rest = rest[8:10], rest[:8] + rest[10:]
    (
        w1_ref,
        w2_ref,
        w3_ref,
        b1_ref,
        b2_ref,
        b3_ref,
        k4_ref,
        b4_ref,
        out_ref,
        clip,
        feats,
        best,
        sim,
        x1,
        x2,
        x3,
        pooled_two,
    ) = rest
    query = lax.axis_index("pb")
    pair = lax.axis_index("slab")
    odd = lax.rem(pair, 2)
    feature_width = feats.shape[-1]
    query_len = qlen_ref[...]
    clip_len = clen_ref[...]

    if n_blocks == 1:
        clip[...] = blocks[0][...]
    else:
        third, first, third_passed, first_passed, one_away, own = blocks
        band = own.shape[1]
        pieces = [(0, own[...]), (1, one_away[...])]
        for at, (direct, passed) in enumerate(((first, first_passed), late, (third, third_passed))):
            for value, k, other in ((direct[0], 0, 1), (passed[1], 1, 0)):
                pieces.append((jnp.where(odd == 0, rounds[k][at], rounds[other][at]), value))
        for k, value in pieces:
            clip[:, pl.ds(pl.multiple_of((query ^ k) * band, band), band), :] = value
    for k, slab in zip(order, slabs):
        rows = slab.shape[1]
        feats[:, pl.ds(pl.multiple_of((pair ^ k) * rows, rows), rows), :] = slab[...]

    flat = feats[...].reshape(regions * frames, feature_width)
    for s in range(0, regions, 2):
        width = min(2, regions - s)
        part = clip[s : s + width].reshape(width * frames, feature_width)
        gram = lax.dot_general(flat, part, (((1,), (1,)), ((), ())), preferred_element_type=F32)
        if width == 2:
            gram = jnp.maximum(gram[:, :frames], gram[:, frames:])
        best[...] = gram if s == 0 else jnp.maximum(best[...], gram)
    total = best[0:frames, :]
    for r in range(1, regions):
        total = total + best[r * frames : (r + 1) * frames, :]
    row = lax.broadcasted_iota(jnp.int32, (frames, frames), 0)
    col = lax.broadcasted_iota(jnp.int32, (frames, frames), 1)
    sim[...] = jnp.where((row < query_len) & (col < clip_len), total * (1.0 / regions), 0.0)

    quarter = frames // 4
    phases = [sim[pl.ds(p, quarter, stride=4), :] for p in range(4)]
    ordered = jnp.concatenate([moved_rows(phases[3], 1), *phases, moved_rows(phases[0], -1)], axis=0)
    windows = frames // 8
    rolled = [pltpu.roll(ordered, 8 * m + 1, 1) for m in range(16)]
    lane = lax.broadcasted_iota(jnp.int32, (frames, LANES), 1)
    for n in range(windows):
        field = None
        for slot in range(5, -1, -1):
            d = slot % 3
            tap = rolled[(2 * slot - n) % 16][d * quarter : d * quarter + frames]
            field = tap if field is None else jnp.where(lane < 16 * slot + 16, tap, field)
        if n == 0:
            field = jnp.where(lane % 16 == 0, 0.0, field)
        if n == windows - 1:
            field = jnp.where(lane % 16 == 9, 0.0, field)
        high = field.astype(BF16)
        low = jnp.where(lane < 48, field - high.astype(F32), field).astype(BF16)
        x1[n * frames : (n + 1) * frames, 0:LANES] = high
        x1[n * frames : (n + 1) * frames, LANES : 2 * LANES] = low
    made = dot(x1[...], w1_ref[...])
    made = jnp.maximum(made[:, :LANES], made[:, LANES:])
    bias_one = jnp.concatenate([b1_ref[...]] * 4, axis=1)
    bias_two = jnp.concatenate([b2_ref[...]] * 2, axis=1)
    first = []
    for n in range(windows):
        here = made[n * frames : (n + 1) * frames]
        halves = []
        for e in range(2):
            pooled = jnp.maximum(
                here[2 * e * quarter : (2 * e + 1) * quarter], here[(2 * e + 1) * quarter : (2 * e + 2) * quarter]
            )
            halves.append(jnp.maximum(pooled + bias_one, 0.0))
        first.append(halves)

    lane = lax.broadcasted_iota(jnp.int32, (quarter, LANES), 1)

    def shifted(parts, width):
        turned = [pltpu.roll(x, width, 1) for x in parts]
        result = []
        for n in range(len(parts) + 1):
            before = turned[n - 1] if n > 0 else jnp.zeros_like(turned[0])
            after = turned[n] if n < len(parts) else jnp.zeros_like(turned[0])
            result.append(jnp.where(lane < width, before, after))
        return result

    even = shifted([x[0] for x in first], 32)
    odds = shifted([x[1] for x in first], 32)
    half = 2 * quarter
    for n in range(windows + 1):
        e, o = even[n], odds[n]
        below, above = moved_rows(o, 1), moved_rows(e, -1)
        if n < windows:
            for d, values in enumerate(((below, e), (e, o), (o, above))):
                high, low = split(jnp.concatenate(values, axis=0))
                x2[n * half : (n + 1) * half, d * LANES : (d + 1) * LANES] = high
                x2[n * half : (n + 1) * half, 640 + d * LANES : 640 + (d + 1) * LANES] = low
        if n > 0:
            base = (n - 1) * half
            packed = (
                jnp.where(lane < 64, below, pltpu.roll(e, 64, 1)),
                jnp.where(lane < 64, e, pltpu.roll(o, 64, 1)),
            )
            for i, values in enumerate((packed, (o, above))):
                high, low = split(jnp.concatenate(values, axis=0))
                at = (3 + i) * LANES
                x2[base : base + half, at : at + LANES] = high
                x2[base : base + half, 640 + at : 640 + at + LANES] = low
    for n in range(0, windows, 2):
        left = x2[n * half : (n + 2) * half, :]
        made = dot(jnp.concatenate([left, left[:, :640], left[:, :640]], axis=1), w2_ref[...])
        made = jnp.maximum(made[:, :LANES], made[:, LANES:])
        for i in range(2):
            here = jnp.maximum(made[i * half : i * half + quarter], made[i * half + quarter : (i + 1) * half])
            pooled_two[n + i] = jnp.maximum(here + bias_two, 0.0)
    second = [pooled_two[n] for n in range(windows)]

    moved = shifted(second, 64)
    for n in range(windows + 1):
        base = n * quarter
        for d, value in enumerate((moved_rows(moved[n], 1), moved[n], moved_rows(moved[n], -1))):
            high, low = split(value)
            x3[base : base + quarter, d * LANES : (d + 1) * LANES] = high
            x3[base : base + quarter, (3 + d) * LANES : (4 + d) * LANES] = low
    bias_four = b4_ref[...]
    row_best = jnp.full((quarter, LANES), -2.0, F32)
    group = 4
    for n in range(0, windows, group):
        left = x3[n * quarter : (n + group) * quarter, :]
        right = x3[(n + 1) * quarter : (n + 1 + group) * quarter, :]
        made = dot(jnp.concatenate([left, right, left[:, :384], right[:, :384]], axis=1), w3_ref[...])
        for c in range(2):
            third = jnp.maximum(made[:, c * LANES : (c + 1) * LANES] + b3_ref[...], 0.0)
            summed = jnp.sum(third * k4_ref[...], axis=1, keepdims=True)
            final = jnp.clip(summed + bias_four, -1.0, 1.0)
            for i in range(group):
                keep = 4 * (2 * (n + i) + c) < clip_len
                row_best = jnp.maximum(row_best, jnp.where(keep, final[i * quarter : (i + 1) * quarter], -2.0))
    row = lax.broadcasted_iota(jnp.int32, (quarter, LANES), 0)
    kept = jnp.where(4 * row < query_len, row_best, 0.0)
    score = jnp.sum(kept, axis=0, keepdims=True) / ((query_len + 3) // 4).astype(F32)
    lane = lax.broadcasted_iota(jnp.int32, out_ref.shape, 1)
    out_ref[...] = jnp.where(lane == pair, score, 0.0)


def per_device(
    query_feats,
    frame_store,
    candidates,
    query_length,
    clip_length,
    kernel_one,
    bias_one,
    kernel_two,
    bias_two,
    kernel_three,
    bias_three,
    kernel_four,
    bias_four,
):
    slab_rows, regions, feature_width = query_feats.shape[1:]
    band = frame_store.shape[1]
    n_query = lax.axis_size("pb")
    n_slab = lax.axis_size("slab")
    frames = band * n_query
    pair_count = candidates.shape[1]
    assert pair_count == n_slab and slab_rows * n_slab == frames == LANES
    vmem = pl.BlockSpec(memory_space=pltpu.VMEM)
    smem = pl.BlockSpec(memory_space=pltpu.SMEM)
    in_hbm = pl.BlockSpec(memory_space=pltpu.HBM)
    store = jnp.transpose(frame_store, (0, 2, 1, 3))
    own = jnp.transpose(query_feats[0], (1, 0, 2))

    def swap(x, k):
        return lax.ppermute(x, "slab", [(s, s ^ k) for s in range(n_slab)])

    rounds = None
    if n_query == 8 and n_slab % 2 == 0:
        rounds = exchange_rounds(n_query)
        steps = len(rounds[0])
        sent = pl.pallas_call(
            functools.partial(pick_kernel, rounds),
            out_shape=[jax.ShapeDtypeStruct((2, *store.shape[1:]), BF16)] * steps
            + [jax.ShapeDtypeStruct(store.shape[1:], BF16)] * 2
            + [jax.ShapeDtypeStruct(own.shape, BF16)],
            in_specs=[in_hbm] * 3,
            out_specs=[vmem] * (steps + 3),
            scratch_shapes=[
                pltpu.SMEM(candidates.T.shape, jnp.int32),
                pltpu.SemaphoreType.DMA((2 * steps + 4,)),
            ],
            compiler_params=pltpu.CompilerParams(vmem_limit_bytes=2 * 1024 * 1024),
            name="pick_bands",
        )(*[pltpu.with_memory_space_constraint(x, pltpu.HBM) for x in (candidates.T, store, own)])
        def cross(at):
            moves = [(q * n_slab + s, (q ^ rounds[s % 2][at]) * n_slab + s) for q in range(n_query) for s in range(n_slab)]
            return lax.ppermute(sent[at], ("pb", "slab"), moves)

        third, first = cross(2), cross(0)
        own = sent[steps + 2]
    else:
        ids = lax.dynamic_index_in_dim(candidates, lax.axis_index("slab"), 1, keepdims=False)
        got = lax.all_to_all(store[ids], "pb", 0, 0, tiled=True)
        blocks = [jnp.transpose(got, (1, 0, 2, 3)).reshape(regions, frames, feature_width)]
    slabs = [own]
    hops = [1 << i for i in range(n_slab.bit_length() - 1)]
    for k in reversed(hops):
        slabs = slabs + [swap(x, k) for x in slabs]
    order = [0]
    for k in reversed(hops):
        order = order + [o ^ k for o in order]
    if rounds is not None:
        one_away = lax.ppermute(sent[steps], "pb", [(q, q ^ 1) for q in range(n_query)])
        blocks = [third, first, swap(third, 1), swap(first, 1), one_away, sent[steps + 1]]

    weights = pl.pallas_call(
        weight_kernel,
        out_shape=[jax.ShapeDtypeStruct((rows, 256), BF16) for rows in (256, 2560, 2304)]
        + [jax.ShapeDtypeStruct((1, LANES), t) for t in (jnp.int32, jnp.int32, F32)],
        in_specs=[vmem] * 3 + [smem] * 4,
        out_specs=[vmem] * 6,
        compiler_params=pltpu.CompilerParams(vmem_limit_bytes=10 * 1024 * 1024),
        cost_estimate=pl.CostEstimate(flops=2_000_000, bytes_accessed=6_000_000, transcendentals=0),
        name="lay_out_kernels",
    )(
        kernel_one.reshape(9, 1, -1),
        kernel_two.reshape(9, 32, 64),
        kernel_three.reshape(9, 64, 128),
        candidates.T,
        query_length,
        clip_length,
        bias_four,
    )
    *weights, query_len, clip_len, last_bias = weights
    late = []
    if rounds is not None:
        second = cross(1)
        second, weights[0] = lax.optimization_barrier((second, weights[0]))
        late = [second, swap(second, 1)]

    vector = pl.pallas_call(
        functools.partial(score_kernel, rounds, len(blocks), order, regions, frames),
        out_shape=jax.ShapeDtypeStruct((1, LANES), F32),
        in_specs=[vmem] * (2 + len(blocks) + len(late) + n_slab + 8),
        out_specs=vmem,
        scratch_shapes=[
            pltpu.VMEM((regions, frames, feature_width), BF16),
            pltpu.VMEM((regions, frames, feature_width), BF16),
            pltpu.VMEM((regions * frames, frames), F32),
            pltpu.VMEM((frames, frames), F32),
            pltpu.VMEM((16 * frames, 256), BF16),
            pltpu.VMEM((16 * 64, 1280), BF16),
            pltpu.VMEM((17 * 32, 768), BF16),
            pltpu.VMEM((16, 32, LANES), F32),
        ],
        compiler_params=pltpu.CompilerParams(vmem_limit_bytes=32 * 1024 * 1024),
        cost_estimate=pl.CostEstimate(flops=2_000_000_000, bytes_accessed=8_000_000, transcendentals=0),
        name="score_pair",
    )(
        query_len,
        clip_len,
        *slabs,
        *blocks,
        *weights,
        bias_one[None],
        bias_two[None],
        bias_three[None],
        kernel_four.reshape(1, -1),
        last_bias,
        *late,
    )
    vector = sum([swap(vector, k) for k in reversed(range(1, n_slab))], vector)
    return vector[:, :pair_count]


def solution(mesh):
    placed = (
        P("pb", "slab", None, None),
        P(None, "pb", None, None),
        P(),
        P("pb"),
        P(),
        P(),
        P(),
        P(),
        P(),
        P(),
        P(),
        P(),
        P(),
    )
    return jax.shard_map(
        per_device, mesh=mesh, in_specs=placed, out_specs=P("pb", None), check_vma=False
    )
```

```python
import functools

import jax
import jax.numpy as jnp
from jax import lax
from jax.experimental import pallas as pl
from jax.experimental.pallas import tpu as pltpu
from jax.sharding import PartitionSpec as P

F32 = jnp.float32
BF16 = jnp.bfloat16
LANES = 128


def exchange_rounds(count):
    odd, even = list(range(count - 1, 1, -2)), list(range(count - 2, 1, -2))
    return odd, [even[1], even[0], *even[2:]]


def split(x):
    high = x.astype(BF16)
    return high, (x - high.astype(F32)).astype(BF16)


def split_three(x):
    high = x.astype(BF16)
    rest = x - high.astype(F32)
    middle = rest.astype(BF16)
    return high, middle, (rest - middle.astype(F32)).astype(BF16)


def pick_kernel(rounds, cand_hbm, store_ref, own_ref, *rest):
    outs, feats, cand_ref, sem = rest[:-3], rest[-3], rest[-2], rest[-1]
    query = lax.axis_index("pb")
    pair = lax.axis_index("slab")
    odd = lax.rem(pair, 2)
    steps = len(rounds[0])
    listed = pltpu.make_async_copy(cand_hbm, cand_ref, sem.at[2 * steps + 3])
    listed.start()
    copies = [pltpu.make_async_copy(own_ref, feats, sem.at[2 * steps + 2])]
    copies[0].start()
    listed.wait()
    for at, out in enumerate(outs):
        if at < steps:
            target = query ^ jnp.where(odd == 0, rounds[0][at], rounds[1][at])
            for part in range(2):
                clip = cand_ref[pair ^ part, target]
                copies.append(pltpu.make_async_copy(store_ref.at[clip], out.at[part], sem.at[2 * at + part]))
        else:
            clip = cand_ref[pair, query ^ (steps + 1 - at)]
            copies.append(pltpu.make_async_copy(store_ref.at[clip], out, sem.at[steps + at]))
    for copy in copies[1:]:
        copy.start()
    for copy in copies:
        copy.wait()


def weight_kernel(
    one_ref,
    two_ref,
    three_ref,
    cand_ref,
    qlen_ref,
    clen_ref,
    b4_ref,
    w1_ref,
    w2_ref,
    w3_ref,
    qlen_out,
    clen_out,
    b4_out,
):
    qlen_out[...] = jnp.full(qlen_out.shape, qlen_ref[0], jnp.int32)
    clip_len = clen_ref[cand_ref[lax.axis_index("slab"), lax.axis_index("pb")]]
    clen_out[...] = jnp.full(clen_out.shape, clip_len, jnp.int32)
    b4_out[...] = jnp.full(b4_out.shape, b4_ref[0], F32)
    row = lax.broadcasted_iota(jnp.int32, (LANES, 256), 0)
    lane = lax.broadcasted_iota(jnp.int32, (LANES, 256), 1)

    def wide(x, times):
        while times > 1:
            x = jnp.concatenate([x, x], axis=1)
            times //= 2
        return x

    def tall(x, times):
        return jnp.concatenate([x] * times, axis=0)

    group = lane // 32
    column = 2 * (group % 4) + group // 4
    slot = row // 16
    total = jnp.zeros((LANES, 256), F32)
    for d in range(3):
        for t in range(3):
            mask = (slot < 6) & (slot % 3 == d) & (row % 16 - column == t)
            total = jnp.where(mask, wide(one_ref[3 * d + t], 8), total)
    high, middle, low = split_three(total)
    for at, part in enumerate((middle, low)):
        both = jnp.where(slot < 3, high.astype(F32), part.astype(F32)).astype(BF16)
        w1_ref[at * LANES : (at + 1) * LANES, :] = both

    def place(ref, base, starts, value):
        for start, part in zip(starts, split_three(value)):
            for s in start:
                ref[s + base : s + base + value.shape[0], :] = part

    group = lane // 64
    column = 2 * (group % 2) + group // 2
    starts = ((0, 640), (1280,), (1920,))
    for d in range(3):
        for first, rows, base in ((0, 128, 128 * d), (4, 64, 384 + 64 * d)):
            total = jnp.zeros((rows, 256), F32)
            for t in range(3):
                tile = tall(wide(two_ref[3 * d + t], 4), rows // 32)
                total = jnp.where((row // 32 + first - column)[:rows] == t, tile, total)
            place(w2_ref, base, starts, total)
    for start in range(0, w2_ref.shape[0], 640):
        w2_ref[start + 576 : start + 640, :] = jnp.zeros((64, 256), BF16)

    column = lane // 128
    for at, first in ((0, 0), (1, 2)):
        for d in range(3):
            total = jnp.zeros((LANES, 256), F32)
            for t in range(3):
                tile = tall(wide(three_ref[3 * d + t], 2), 2)
                total = jnp.where(row // 64 + first - column == t, tile, total)
            place(w3_ref, LANES * d, ((768 * at, 768 * at + 384), (1536 + 384 * at,)), total)


def moved_rows(x, step):
    rows = x.shape[0]
    row = lax.broadcasted_iota(jnp.int32, x.shape, 0)
    if step == 1:
        return jnp.where(row == 0, 0.0, pltpu.roll(x, 1, 0))
    return jnp.where(row == rows - 1, 0.0, pltpu.roll(x, rows - 1, 0))


def dot(a, b):
    return jnp.dot(a, b, preferred_element_type=F32)


def score_kernel(
    rounds,
    n_blocks,
    order,
    regions,
    frames,
    qlen_ref,
    clen_ref,
    *rest,
):
    n_slabs = len(order)
    slabs, rest = rest[:n_slabs], rest[n_slabs:]
    blocks, rest = rest[:n_blocks], rest[n_blocks:]
    late = ()
    if n_blocks > 1:
        late, rest = rest[8:10], rest[:8] + rest[10:]
    (
        w1_ref,
        w2_ref,
        w3_ref,
        b1_ref,
        b2_ref,
        b3_ref,
        k4_ref,
        b4_ref,
        out_ref,
        clip,
        feats,
        best,
        sim,
        x1,
        x2,
        x3,
        pooled_two,
    ) = rest
    query = lax.axis_index("pb")
    pair = lax.axis_index("slab")
    odd = lax.rem(pair, 2)
    feature_width = feats.shape[-1]
    query_len = qlen_ref[...]
    clip_len = clen_ref[...]

    if n_blocks == 1:
        clip[...] = blocks[0][...]
    else:
        third, first, third_passed, first_passed, one_away, own = blocks
        band = own.shape[1]
        pieces = [(0, own[...]), (1, one_away[...])]
        for at, (direct, passed) in enumerate(((first, first_passed), late, (third, third_passed))):
            for value, k, other in ((direct[0], 0, 1), (passed[1], 1, 0)):
                pieces.append((jnp.where(odd == 0, rounds[k][at], rounds[other][at]), value))
        for k, value in pieces:
            clip[:, pl.ds(pl.multiple_of((query ^ k) * band, band), band), :] = value
    for k, slab in zip(order, slabs):
        rows = slab.shape[1]
        feats[:, pl.ds(pl.multiple_of((pair ^ k) * rows, rows), rows), :] = slab[...]

    flat = feats[...].reshape(regions * frames, feature_width)
    for s in range(0, regions, 2):
        width = min(2, regions - s)
        part = clip[s : s + width].reshape(width * frames, feature_width)
        gram = lax.dot_general(flat, part, (((1,), (1,)), ((), ())), preferred_element_type=F32)
        if width == 2:
            gram = jnp.maximum(gram[:, :frames], gram[:, frames:])
        best[...] = gram if s == 0 else jnp.maximum(best[...], gram)
    total = best[0:frames, :]
    for r in range(1, regions):
        total = total + best[r * frames : (r + 1) * frames, :]
    row = lax.broadcasted_iota(jnp.int32, (frames, frames), 0)
    col = lax.broadcasted_iota(jnp.int32, (frames, frames), 1)
    sim[...] = jnp.where((row < query_len) & (col < clip_len), total * (1.0 / regions), 0.0)

    quarter = frames // 4
    phases = [sim[pl.ds(p, quarter, stride=4), :] for p in range(4)]
    ordered = jnp.concatenate([moved_rows(phases[3], 1), *phases, moved_rows(phases[0], -1)], axis=0)
    windows = frames // 8
    rolled = [pltpu.roll(ordered, 8 * m + 1, 1) for m in range(16)]
    lane = lax.broadcasted_iota(jnp.int32, (frames, LANES), 1)
    chunks = []
    for n in range(windows):
        field = None
        for slot in range(5, -1, -1):
            d = slot % 3
            tap = rolled[(2 * slot - n) % 16][d * quarter : d * quarter + frames]
            field = tap if field is None else jnp.where(lane < 16 * slot + 16, tap, field)
        if n == 0:
            field = jnp.where(lane % 16 == 0, 0.0, field)
        if n == windows - 1:
            field = jnp.where(lane % 16 == 9, 0.0, field)
        high = field.astype(BF16)
        low = jnp.where(lane < 48, field - high.astype(F32), field).astype(BF16)
        x1[n * frames : (n + 1) * frames, 0:LANES] = high
        x1[n * frames : (n + 1) * frames, LANES : 2 * LANES] = low
        if n % 4 == 3:
            made = dot(x1[(n - 3) * frames : (n + 1) * frames, :], w1_ref[...])
            chunks.append(jnp.maximum(made[:, :LANES], made[:, LANES:]))
    bias_one = jnp.concatenate([b1_ref[...]] * 4, axis=1)
    bias_two = jnp.concatenate([b2_ref[...]] * 2, axis=1)
    first = []
    for n in range(windows):
        here = chunks[n // 4][n % 4 * frames : (n % 4 + 1) * frames]
        halves = []
        for e in range(2):
            pooled = jnp.maximum(
                here[2 * e * quarter : (2 * e + 1) * quarter], here[(2 * e + 1) * quarter : (2 * e + 2) * quarter]
            )
            halves.append(jnp.maximum(pooled + bias_one, 0.0))
        first.append(halves)

    lane = lax.broadcasted_iota(jnp.int32, (quarter, LANES), 1)

    def shifted(parts, width):
        turned = [pltpu.roll(x, width, 1) for x in parts]
        result = []
        for n in range(len(parts) + 1):
            before = turned[n - 1] if n > 0 else jnp.zeros_like(turned[0])
            after = turned[n] if n < len(parts) else jnp.zeros_like(turned[0])
            result.append(jnp.where(lane < width, before, after))
        return result

    even = shifted([x[0] for x in first], 32)
    odds = shifted([x[1] for x in first], 32)
    half = 2 * quarter
    for n in range(windows + 1):
        e, o = even[n], odds[n]
        below, above = moved_rows(o, 1), moved_rows(e, -1)
        if n < windows:
            for d, values in enumerate(((below, e), (e, o), (o, above))):
                high, low = split(jnp.concatenate(values, axis=0))
                x2[n * half : (n + 1) * half, d * LANES : (d + 1) * LANES] = high
                x2[n * half : (n + 1) * half, 640 + d * LANES : 640 + (d + 1) * LANES] = low
        if n > 0:
            base = (n - 1) * half
            packed = (
                jnp.where(lane < 64, below, pltpu.roll(e, 64, 1)),
                jnp.where(lane < 64, e, pltpu.roll(o, 64, 1)),
            )
            for i, values in enumerate((packed, (o, above))):
                high, low = split(jnp.concatenate(values, axis=0))
                at = (3 + i) * LANES
                x2[base : base + half, at : at + LANES] = high
                x2[base : base + half, 640 + at : 640 + at + LANES] = low
    for n in range(0, windows, 2):
        left = x2[n * half : (n + 2) * half, :]
        made = dot(jnp.concatenate([left, left[:, :640], left[:, :640]], axis=1), w2_ref[...])
        made = jnp.maximum(made[:, :LANES], made[:, LANES:])
        for i in range(2):
            here = jnp.maximum(made[i * half : i * half + quarter], made[i * half + quarter : (i + 1) * half])
            pooled_two[n + i] = jnp.maximum(here + bias_two, 0.0)
    second = [pooled_two[n] for n in range(windows)]

    moved = shifted(second, 64)
    for n in range(windows + 1):
        base = n * quarter
        for d, value in enumerate((moved_rows(moved[n], 1), moved[n], moved_rows(moved[n], -1))):
            high, low = split(value)
            x3[base : base + quarter, d * LANES : (d + 1) * LANES] = high
            x3[base : base + quarter, (3 + d) * LANES : (4 + d) * LANES] = low
    bias_four = b4_ref[...]
    row_best = jnp.full((quarter, LANES), -2.0, F32)
    group = 4
    for n in range(0, windows, group):
        left = x3[n * quarter : (n + group) * quarter, :]
        right = x3[(n + 1) * quarter : (n + 1 + group) * quarter, :]
        made = dot(jnp.concatenate([left, right, left[:, :384], right[:, :384]], axis=1), w3_ref[...])
        for c in range(2):
            third = jnp.maximum(made[:, c * LANES : (c + 1) * LANES] + b3_ref[...], 0.0)
            summed = jnp.sum(third * k4_ref[...], axis=1, keepdims=True)
            final = jnp.clip(summed + bias_four, -1.0, 1.0)
            for i in range(group):
                keep = 4 * (2 * (n + i) + c) < clip_len
                row_best = jnp.maximum(row_best, jnp.where(keep, final[i * quarter : (i + 1) * quarter], -2.0))
    row = lax.broadcasted_iota(jnp.int32, (quarter, LANES), 0)
    kept = jnp.where(4 * row < query_len, row_best, 0.0)
    score = jnp.sum(kept, axis=0, keepdims=True) / ((query_len + 3) // 4).astype(F32)
    lane = lax.broadcasted_iota(jnp.int32, out_ref.shape, 1)
    out_ref[...] = jnp.where(lane == pair, score, 0.0)


def per_device(
    query_feats,
    frame_store,
    candidates,
    query_length,
    clip_length,
    kernel_one,
    bias_one,
    kernel_two,
    bias_two,
    kernel_three,
    bias_three,
    kernel_four,
    bias_four,
):
    slab_rows, regions, feature_width = query_feats.shape[1:]
    band = frame_store.shape[1]
    n_query = lax.axis_size("pb")
    n_slab = lax.axis_size("slab")
    frames = band * n_query
    pair_count = candidates.shape[1]
    assert pair_count == n_slab and slab_rows * n_slab == frames == LANES
    vmem = pl.BlockSpec(memory_space=pltpu.VMEM)
    smem = pl.BlockSpec(memory_space=pltpu.SMEM)
    in_hbm = pl.BlockSpec(memory_space=pltpu.HBM)
    store = jnp.transpose(frame_store, (0, 2, 1, 3))
    own = jnp.transpose(query_feats[0], (1, 0, 2))

    def swap(x, k):
        return lax.ppermute(x, "slab", [(s, s ^ k) for s in range(n_slab)])

    rounds = None
    if n_query == 8 and n_slab % 2 == 0:
        rounds = exchange_rounds(n_query)
        steps = len(rounds[0])
        sent = pl.pallas_call(
            functools.partial(pick_kernel, rounds),
            out_shape=[jax.ShapeDtypeStruct((2, *store.shape[1:]), BF16)] * steps
            + [jax.ShapeDtypeStruct(store.shape[1:], BF16)] * 2
            + [jax.ShapeDtypeStruct(own.shape, BF16)],
            in_specs=[in_hbm] * 3,
            out_specs=[vmem] * (steps + 3),
            scratch_shapes=[
                pltpu.SMEM(candidates.T.shape, jnp.int32),
                pltpu.SemaphoreType.DMA((2 * steps + 4,)),
            ],
            compiler_params=pltpu.CompilerParams(vmem_limit_bytes=2 * 1024 * 1024),
            name="pick_bands",
        )(*[pltpu.with_memory_space_constraint(x, pltpu.HBM) for x in (candidates.T, store, own)])
        def cross(at):
            moves = [(q * n_slab + s, (q ^ rounds[s % 2][at]) * n_slab + s) for q in range(n_query) for s in range(n_slab)]
            return lax.ppermute(sent[at], ("pb", "slab"), moves)

        third, first = cross(2), cross(0)
        own = sent[steps + 2]
    else:
        ids = lax.dynamic_index_in_dim(candidates, lax.axis_index("slab"), 1, keepdims=False)
        got = lax.all_to_all(store[ids], "pb", 0, 0, tiled=True)
        blocks = [jnp.transpose(got, (1, 0, 2, 3)).reshape(regions, frames, feature_width)]
    slabs = [own]
    hops = [1 << i for i in range(n_slab.bit_length() - 1)]
    for k in reversed(hops):
        slabs = slabs + [swap(x, k) for x in slabs]
    order = [0]
    for k in reversed(hops):
        order = order + [o ^ k for o in order]
    if rounds is not None:
        one_away = lax.ppermute(sent[steps], "pb", [(q, q ^ 1) for q in range(n_query)])
        blocks = [third, first, swap(third, 1), swap(first, 1), one_away, sent[steps + 1]]

    weights = pl.pallas_call(
        weight_kernel,
        out_shape=[jax.ShapeDtypeStruct((rows, 256), BF16) for rows in (256, 2560, 2304)]
        + [jax.ShapeDtypeStruct((1, LANES), t) for t in (jnp.int32, jnp.int32, F32)],
        in_specs=[vmem] * 3 + [smem] * 4,
        out_specs=[vmem] * 6,
        compiler_params=pltpu.CompilerParams(vmem_limit_bytes=10 * 1024 * 1024),
        cost_estimate=pl.CostEstimate(flops=2_000_000, bytes_accessed=6_000_000, transcendentals=0),
        name="lay_out_kernels",
    )(
        kernel_one.reshape(9, 1, -1),
        kernel_two.reshape(9, 32, 64),
        kernel_three.reshape(9, 64, 128),
        candidates.T,
        query_length,
        clip_length,
        bias_four,
    )
    *weights, query_len, clip_len, last_bias = weights
    late = []
    if rounds is not None:
        second = cross(1)
        second, weights[0] = lax.optimization_barrier((second, weights[0]))
        late = [second, swap(second, 1)]

    vector = pl.pallas_call(
        functools.partial(score_kernel, rounds, len(blocks), order, regions, frames),
        out_shape=jax.ShapeDtypeStruct((1, LANES), F32),
        in_specs=[vmem] * (2 + len(blocks) + len(late) + n_slab + 8),
        out_specs=vmem,
        scratch_shapes=[
            pltpu.VMEM((regions, frames, feature_width), BF16),
            pltpu.VMEM((regions, frames, feature_width), BF16),
            pltpu.VMEM((regions * frames, frames), F32),
            pltpu.VMEM((frames, frames), F32),
            pltpu.VMEM((16 * frames, 256), BF16),
            pltpu.VMEM((16 * 64, 1280), BF16),
            pltpu.VMEM((17 * 32, 768), BF16),
            pltpu.VMEM((16, 32, LANES), F32),
        ],
        compiler_params=pltpu.CompilerParams(vmem_limit_bytes=32 * 1024 * 1024),
        cost_estimate=pl.CostEstimate(flops=2_000_000_000, bytes_accessed=8_000_000, transcendentals=0),
        name="score_pair",
    )(
        query_len,
        clip_len,
        *slabs,
        *blocks,
        *weights,
        bias_one[None],
        bias_two[None],
        bias_three[None],
        kernel_four.reshape(1, -1),
        last_bias,
        *late,
    )
    vector = sum([swap(vector, k) for k in reversed(range(1, n_slab))], vector)
    return vector[:, :pair_count]


def solution(mesh):
    placed = (
        P("pb", "slab", None, None),
        P(None, "pb", None, None),
        P(),
        P("pb"),
        P(),
        P(),
        P(),
        P(),
        P(),
        P(),
        P(),
        P(),
        P(),
    )
    return jax.shard_map(
        per_device, mesh=mesh, in_specs=placed, out_specs=P("pb", None), check_vma=False
    )
```

```python
import functools

import jax
import jax.numpy as jnp
from jax import lax
from jax.experimental import pallas as pl
from jax.experimental.pallas import tpu as pltpu
from jax.sharding import PartitionSpec as P

F32 = jnp.float32
BF16 = jnp.bfloat16
LANES = 128


def exchange_rounds(count):
    odd, even = list(range(count - 1, 1, -2)), list(range(count - 2, 1, -2))
    return odd, [even[1], even[0], *even[2:]]


def split(x):
    high = x.astype(BF16)
    return high, (x - high.astype(F32)).astype(BF16)


def split_three(x):
    high = x.astype(BF16)
    rest = x - high.astype(F32)
    middle = rest.astype(BF16)
    return high, middle, (rest - middle.astype(F32)).astype(BF16)


def pick_kernel(rounds, cand_hbm, store_ref, own_ref, *rest):
    outs, feats, cand_ref, sem = rest[:-3], rest[-3], rest[-2], rest[-1]
    query = lax.axis_index("pb")
    pair = lax.axis_index("slab")
    odd = lax.rem(pair, 2)
    steps = len(rounds[0])
    listed = pltpu.make_async_copy(cand_hbm, cand_ref, sem.at[2 * steps + 3])
    listed.start()
    copies = [pltpu.make_async_copy(own_ref, feats, sem.at[2 * steps + 2])]
    copies[0].start()
    listed.wait()
    for at, out in enumerate(outs):
        if at < steps:
            target = query ^ jnp.where(odd == 0, rounds[0][at], rounds[1][at])
            for part in range(2):
                clip = cand_ref[pair ^ part, target]
                copies.append(pltpu.make_async_copy(store_ref.at[clip], out.at[part], sem.at[2 * at + part]))
        else:
            clip = cand_ref[pair, query ^ (steps + 1 - at)]
            copies.append(pltpu.make_async_copy(store_ref.at[clip], out, sem.at[steps + at]))
    for copy in copies[1:]:
        copy.start()
    for copy in copies:
        copy.wait()


def weight_kernel(
    one_ref,
    two_ref,
    three_ref,
    cand_ref,
    qlen_ref,
    clen_ref,
    b4_ref,
    w1_ref,
    w2_ref,
    w3_ref,
    qlen_out,
    clen_out,
    b4_out,
):
    qlen_out[...] = jnp.full(qlen_out.shape, qlen_ref[0], jnp.int32)
    clip_len = clen_ref[cand_ref[lax.axis_index("slab"), lax.axis_index("pb")]]
    clen_out[...] = jnp.full(clen_out.shape, clip_len, jnp.int32)
    b4_out[...] = jnp.full(b4_out.shape, b4_ref[0], F32)
    row = lax.broadcasted_iota(jnp.int32, (LANES, 256), 0)
    lane = lax.broadcasted_iota(jnp.int32, (LANES, 256), 1)

    def wide(x, times):
        while times > 1:
            x = jnp.concatenate([x, x], axis=1)
            times //= 2
        return x

    def tall(x, times):
        return jnp.concatenate([x] * times, axis=0)

    group = lane // 32
    column = 2 * (group % 4) + group // 4
    slot = row // 16
    total = jnp.zeros((LANES, 256), F32)
    for d in range(3):
        for t in range(3):
            mask = (slot < 6) & (slot % 3 == d) & (row % 16 - column == t)
            total = jnp.where(mask, wide(one_ref[3 * d + t], 8), total)
    high, middle, low = split_three(total)
    for at, part in enumerate((middle, low)):
        both = jnp.where(slot < 3, high.astype(F32), part.astype(F32)).astype(BF16)
        w1_ref[at * LANES : (at + 1) * LANES, :] = both

    def place(ref, base, starts, value):
        for start, part in zip(starts, split_three(value)):
            for s in start:
                ref[s + base : s + base + value.shape[0], :] = part

    group = lane // 64
    column = 2 * (group % 2) + group // 2
    starts = ((0, 640), (1280,), (1920,))
    for d in range(3):
        for first, rows, base in ((0, 128, 128 * d), (4, 64, 384 + 64 * d)):
            total = jnp.zeros((rows, 256), F32)
            for t in range(3):
                tile = tall(wide(two_ref[3 * d + t], 4), rows // 32)
                total = jnp.where((row // 32 + first - column)[:rows] == t, tile, total)
            place(w2_ref, base, starts, total)
    for start in range(0, w2_ref.shape[0], 640):
        w2_ref[start + 576 : start + 640, :] = jnp.zeros((64, 256), BF16)

    column = lane // 128
    for at, first in ((0, 0), (1, 2)):
        for d in range(3):
            total = jnp.zeros((LANES, 256), F32)
            for t in range(3):
                tile = tall(wide(three_ref[3 * d + t], 2), 2)
                total = jnp.where(row // 64 + first - column == t, tile, total)
            place(w3_ref, LANES * d, ((768 * at, 768 * at + 384), (1536 + 384 * at,)), total)


def moved_rows(x, step):
    rows = x.shape[0]
    row = lax.broadcasted_iota(jnp.int32, x.shape, 0)
    if step == 1:
        return jnp.where(row == 0, 0.0, pltpu.roll(x, 1, 0))
    return jnp.where(row == rows - 1, 0.0, pltpu.roll(x, rows - 1, 0))


def dot(a, b):
    return jnp.dot(a, b, preferred_element_type=F32)


def score_kernel(
    rounds,
    n_blocks,
    order,
    regions,
    frames,
    qlen_ref,
    clen_ref,
    *rest,
):
    n_slabs = len(order)
    slabs, rest = rest[:n_slabs], rest[n_slabs:]
    blocks, rest = rest[:n_blocks], rest[n_blocks:]
    late = ()
    if n_blocks > 1:
        late, rest = rest[8:10], rest[:8] + rest[10:]
    (
        w1_ref,
        w2_ref,
        w3_ref,
        b1_ref,
        b2_ref,
        b3_ref,
        k4_ref,
        b4_ref,
        out_ref,
        clip,
        feats,
        best,
        sim,
        x1,
        x2,
        x3,
        pooled_two,
    ) = rest
    query = lax.axis_index("pb")
    pair = lax.axis_index("slab")
    odd = lax.rem(pair, 2)
    feature_width = feats.shape[-1]
    query_len = qlen_ref[...]
    clip_len = clen_ref[...]

    if n_blocks == 1:
        clip[...] = blocks[0][...]
    else:
        third, first, third_passed, first_passed, one_away, own = blocks
        band = own.shape[1]
        pieces = [(0, own[...]), (1, one_away[...])]
        for at, (direct, passed) in enumerate(((first, first_passed), late, (third, third_passed))):
            for value, k, other in ((direct[0], 0, 1), (passed[1], 1, 0)):
                pieces.append((jnp.where(odd == 0, rounds[k][at], rounds[other][at]), value))
        for k, value in pieces:
            clip[:, pl.ds(pl.multiple_of((query ^ k) * band, band), band), :] = value
    for k, slab in zip(order, slabs):
        rows = slab.shape[1]
        feats[:, pl.ds(pl.multiple_of((pair ^ k) * rows, rows), rows), :] = slab[...]

    flat = feats[...].reshape(regions * frames, feature_width)
    for s in range(0, regions, 2):
        width = min(2, regions - s)
        part = clip[s : s + width].reshape(width * frames, feature_width)
        gram = lax.dot_general(flat, part, (((1,), (1,)), ((), ())), preferred_element_type=F32)
        if width == 2:
            gram = jnp.maximum(gram[:, :frames], gram[:, frames:])
        best[...] = gram if s == 0 else jnp.maximum(best[...], gram)
    total = best[0:frames, :]
    for r in range(1, regions):
        total = total + best[r * frames : (r + 1) * frames, :]
    row = lax.broadcasted_iota(jnp.int32, (frames, frames), 0)
    col = lax.broadcasted_iota(jnp.int32, (frames, frames), 1)
    sim[...] = jnp.where((row < query_len) & (col < clip_len), total * (1.0 / regions), 0.0)

    quarter = frames // 4
    phases = [sim[pl.ds(p, quarter, stride=4), :] for p in range(4)]
    ordered = jnp.concatenate([moved_rows(phases[3], 1), *phases, moved_rows(phases[0], -1)], axis=0)
    windows = frames // 8
    rolled = [pltpu.roll(ordered, 8 * m + 1, 1) for m in range(16)]
    lane = lax.broadcasted_iota(jnp.int32, (frames, LANES), 1)
    chunks = []
    for n in range(windows):
        field = None
        for slot in range(5, -1, -1):
            d = slot % 3
            tap = rolled[(2 * slot - n) % 16][d * quarter : d * quarter + frames]
            field = tap if field is None else jnp.where(lane < 16 * slot + 16, tap, field)
        if n == 0:
            field = jnp.where(lane % 16 == 0, 0.0, field)
        if n == windows - 1:
            field = jnp.where(lane % 16 == 9, 0.0, field)
        high = field.astype(BF16)
        low = jnp.where(lane < 48, field - high.astype(F32), field).astype(BF16)
        x1[n * frames : (n + 1) * frames, 0:LANES] = high
        x1[n * frames : (n + 1) * frames, LANES : 2 * LANES] = low
        if n % 4 == 3:
            made = dot(x1[(n - 3) * frames : (n + 1) * frames, :], w1_ref[...])
            chunks.append(jnp.maximum(made[:, :LANES], made[:, LANES:]))
    bias_one = jnp.concatenate([b1_ref[...]] * 4, axis=1)
    bias_two = jnp.concatenate([b2_ref[...]] * 2, axis=1)
    first = []
    for n in range(windows):
        here = chunks[n // 4][n % 4 * frames : (n % 4 + 1) * frames]
        halves = []
        for e in range(2):
            pooled = jnp.maximum(
                here[2 * e * quarter : (2 * e + 1) * quarter], here[(2 * e + 1) * quarter : (2 * e + 2) * quarter]
            )
            halves.append(jnp.maximum(pooled + bias_one, 0.0))
        first.append(halves)

    lane = lax.broadcasted_iota(jnp.int32, (quarter, LANES), 1)

    def shifted(parts, width):
        turned = [pltpu.roll(x, width, 1) for x in parts]
        result = []
        for n in range(len(parts) + 1):
            before = turned[n - 1] if n > 0 else jnp.zeros_like(turned[0])
            after = turned[n] if n < len(parts) else jnp.zeros_like(turned[0])
            result.append(jnp.where(lane < width, before, after))
        return result

    even = shifted([x[0] for x in first], 32)
    odds = shifted([x[1] for x in first], 32)
    half = 2 * quarter
    for n in range(windows + 1):
        e, o = even[n], odds[n]
        below, above = moved_rows(o, 1), moved_rows(e, -1)
        if n < windows:
            for d, values in enumerate(((below, e), (e, o), (o, above))):
                high, low = split(jnp.concatenate(values, axis=0))
                x2[n * half : (n + 1) * half, d * LANES : (d + 1) * LANES] = high
                x2[n * half : (n + 1) * half, 640 + d * LANES : 640 + (d + 1) * LANES] = low
        if n > 0:
            base = (n - 1) * half
            packed = (
                jnp.where(lane < 64, below, pltpu.roll(e, 64, 1)),
                jnp.where(lane < 64, e, pltpu.roll(o, 64, 1)),
            )
            for i, values in enumerate((packed, (o, above))):
                high, low = split(jnp.concatenate(values, axis=0))
                at = (3 + i) * LANES
                x2[base : base + half, at : at + LANES] = high
                x2[base : base + half, 640 + at : 640 + at + LANES] = low
        if n > 0 and n % 2 == 0:
            left = x2[(n - 2) * half : n * half, :]
            made = dot(jnp.concatenate([left, left[:, :640], left[:, :640]], axis=1), w2_ref[...])
            made = jnp.maximum(made[:, :LANES], made[:, LANES:])
            for i in range(2):
                here = jnp.maximum(made[i * half : i * half + quarter], made[i * half + quarter : (i + 1) * half])
                pooled_two[n - 2 + i] = jnp.maximum(here + bias_two, 0.0)
    second = [pooled_two[n] for n in range(windows)]

    moved = shifted(second, 64)
    for n in range(windows + 1):
        base = n * quarter
        for d, value in enumerate((moved_rows(moved[n], 1), moved[n], moved_rows(moved[n], -1))):
            high, low = split(value)
            x3[base : base + quarter, d * LANES : (d + 1) * LANES] = high
            x3[base : base + quarter, (3 + d) * LANES : (4 + d) * LANES] = low
    bias_four = b4_ref[...]
    row_best = jnp.full((quarter, LANES), -2.0, F32)
    group = 4
    for n in range(0, windows, group):
        left = x3[n * quarter : (n + group) * quarter, :]
        right = x3[(n + 1) * quarter : (n + 1 + group) * quarter, :]
        made = dot(jnp.concatenate([left, right, left[:, :384], right[:, :384]], axis=1), w3_ref[...])
        for c in range(2):
            third = jnp.maximum(made[:, c * LANES : (c + 1) * LANES] + b3_ref[...], 0.0)
            summed = jnp.sum(third * k4_ref[...], axis=1, keepdims=True)
            final = jnp.clip(summed + bias_four, -1.0, 1.0)
            for i in range(group):
                keep = 4 * (2 * (n + i) + c) < clip_len
                row_best = jnp.maximum(row_best, jnp.where(keep, final[i * quarter : (i + 1) * quarter], -2.0))
    row = lax.broadcasted_iota(jnp.int32, (quarter, LANES), 0)
    kept = jnp.where(4 * row < query_len, row_best, 0.0)
    score = jnp.sum(kept, axis=0, keepdims=True) / ((query_len + 3) // 4).astype(F32)
    lane = lax.broadcasted_iota(jnp.int32, out_ref.shape, 1)
    out_ref[...] = jnp.where(lane == pair, score, 0.0)


def per_device(
    query_feats,
    frame_store,
    candidates,
    query_length,
    clip_length,
    kernel_one,
    bias_one,
    kernel_two,
    bias_two,
    kernel_three,
    bias_three,
    kernel_four,
    bias_four,
):
    slab_rows, regions, feature_width = query_feats.shape[1:]
    band = frame_store.shape[1]
    n_query = lax.axis_size("pb")
    n_slab = lax.axis_size("slab")
    frames = band * n_query
    pair_count = candidates.shape[1]
    assert pair_count == n_slab and slab_rows * n_slab == frames == LANES
    vmem = pl.BlockSpec(memory_space=pltpu.VMEM)
    smem = pl.BlockSpec(memory_space=pltpu.SMEM)
    in_hbm = pl.BlockSpec(memory_space=pltpu.HBM)
    store = jnp.transpose(frame_store, (0, 2, 1, 3))
    own = jnp.transpose(query_feats[0], (1, 0, 2))

    def swap(x, k):
        return lax.ppermute(x, "slab", [(s, s ^ k) for s in range(n_slab)])

    rounds = None
    if n_query == 8 and n_slab % 2 == 0:
        rounds = exchange_rounds(n_query)
        steps = len(rounds[0])
        sent = pl.pallas_call(
            functools.partial(pick_kernel, rounds),
            out_shape=[jax.ShapeDtypeStruct((2, *store.shape[1:]), BF16)] * steps
            + [jax.ShapeDtypeStruct(store.shape[1:], BF16)] * 2
            + [jax.ShapeDtypeStruct(own.shape, BF16)],
            in_specs=[in_hbm] * 3,
            out_specs=[vmem] * (steps + 3),
            scratch_shapes=[
                pltpu.SMEM(candidates.T.shape, jnp.int32),
                pltpu.SemaphoreType.DMA((2 * steps + 4,)),
            ],
            compiler_params=pltpu.CompilerParams(vmem_limit_bytes=2 * 1024 * 1024),
            name="pick_bands",
        )(*[pltpu.with_memory_space_constraint(x, pltpu.HBM) for x in (candidates.T, store, own)])
        def cross(at):
            moves = [(q * n_slab + s, (q ^ rounds[s % 2][at]) * n_slab + s) for q in range(n_query) for s in range(n_slab)]
            return lax.ppermute(sent[at], ("pb", "slab"), moves)

        third, first = cross(2), cross(0)
        own = sent[steps + 2]
    else:
        ids = lax.dynamic_index_in_dim(candidates, lax.axis_index("slab"), 1, keepdims=False)
        got = lax.all_to_all(store[ids], "pb", 0, 0, tiled=True)
        blocks = [jnp.transpose(got, (1, 0, 2, 3)).reshape(regions, frames, feature_width)]
    slabs = [own]
    hops = [1 << i for i in range(n_slab.bit_length() - 1)]
    for k in reversed(hops):
        slabs = slabs + [swap(x, k) for x in slabs]
    order = [0]
    for k in reversed(hops):
        order = order + [o ^ k for o in order]
    if rounds is not None:
        one_away = lax.ppermute(sent[steps], "pb", [(q, q ^ 1) for q in range(n_query)])
        blocks = [third, first, swap(third, 1), swap(first, 1), one_away, sent[steps + 1]]

    weights = pl.pallas_call(
        weight_kernel,
        out_shape=[jax.ShapeDtypeStruct((rows, 256), BF16) for rows in (256, 2560, 2304)]
        + [jax.ShapeDtypeStruct((1, LANES), t) for t in (jnp.int32, jnp.int32, F32)],
        in_specs=[vmem] * 3 + [smem] * 4,
        out_specs=[vmem] * 6,
        compiler_params=pltpu.CompilerParams(vmem_limit_bytes=10 * 1024 * 1024),
        cost_estimate=pl.CostEstimate(flops=2_000_000, bytes_accessed=6_000_000, transcendentals=0),
        name="lay_out_kernels",
    )(
        kernel_one.reshape(9, 1, -1),
        kernel_two.reshape(9, 32, 64),
        kernel_three.reshape(9, 64, 128),
        candidates.T,
        query_length,
        clip_length,
        bias_four,
    )
    *weights, query_len, clip_len, last_bias = weights
    late = []
    if rounds is not None:
        second = cross(1)
        second, weights[0] = lax.optimization_barrier((second, weights[0]))
        late = [second, swap(second, 1)]

    vector = pl.pallas_call(
        functools.partial(score_kernel, rounds, len(blocks), order, regions, frames),
        out_shape=jax.ShapeDtypeStruct((1, LANES), F32),
        in_specs=[vmem] * (2 + len(blocks) + len(late) + n_slab + 8),
        out_specs=vmem,
        scratch_shapes=[
            pltpu.VMEM((regions, frames, feature_width), BF16),
            pltpu.VMEM((regions, frames, feature_width), BF16),
            pltpu.VMEM((regions * frames, frames), F32),
            pltpu.VMEM((frames, frames), F32),
            pltpu.VMEM((16 * frames, 256), BF16),
            pltpu.VMEM((16 * 64, 1280), BF16),
            pltpu.VMEM((17 * 32, 768), BF16),
            pltpu.VMEM((16, 32, LANES), F32),
        ],
        compiler_params=pltpu.CompilerParams(vmem_limit_bytes=32 * 1024 * 1024),
        cost_estimate=pl.CostEstimate(flops=2_000_000_000, bytes_accessed=8_000_000, transcendentals=0),
        name="score_pair",
    )(
        query_len,
        clip_len,
        *slabs,
        *blocks,
        *weights,
        bias_one[None],
        bias_two[None],
        bias_three[None],
        kernel_four.reshape(1, -1),
        last_bias,
        *late,
    )
    vector = sum([swap(vector, k) for k in reversed(range(1, n_slab))], vector)
    return vector[:, :pair_count]


def solution(mesh):
    placed = (
        P("pb", "slab", None, None),
        P(None, "pb", None, None),
        P(),
        P("pb"),
        P(),
        P(),
        P(),
        P(),
        P(),
        P(),
        P(),
        P(),
        P(),
    )
    return jax.shard_map(
        per_device, mesh=mesh, in_specs=placed, out_specs=P("pb", None), check_vma=False
    )
```
